32 devices in a mesh: groups: 2 (over x), role: 1, tp: 16 (over z, y, core).
Axes of the slice: x: 2, y: 2, z: 4, core: 2. Of those that a mesh axis runs over, the one named last changes fastest.
Arguments:
- queries: bfloat16 [4, 64, 16384], P(('groups', 'role'), None, 'tp'), parts along dimension 0, may hold values from -18 to 18
- cache_keys: bfloat16 [4, 16384, 1024], P(('groups', 'role'), 'tp'), parts along dimension 0, may hold values from -6 to 6
- cache_values: bfloat16 [4, 16384, 1024], P(('groups', 'role'), 'tp'), parts along dimension 0, may hold values from -6 to 6
- fresh_keys: bfloat16 [4, 64, 1024], P(('groups', 'role'), None, 'tp'), parts along dimension 0, may hold values from -12 to 12
- fresh_values: bfloat16 [4, 64, 1024], P(('groups', 'role'), None, 'tp'), parts along dimension 0, may hold values from -6 to 6
- prefill_prefixes: int32 [8], P('groups'), parts along dimension 0, may hold values from 1 to 6144, 16384 in all
- decode_prefixes: int32 [64], P('groups'), parts along dimension 0, may hold values from 1 to 8192, 16384 in all
- prefill_counts: int32 [8], P('groups'), parts along dimension 0, may hold values from 1 to 32, 64 in all
Outputs:
- attended: bfloat16 [4, 64, 16384], P(('groups', 'role'), None, 'tp'), parts along dimension 0
- handed_keys: bfloat16 [4, 64, 1024], P(('groups', 'role'), 'tp'), parts along dimension 0
- handed_values: bfloat16 [4, 64, 1024], P(('groups', 'role'), 'tp'), parts along dimension 0
The draws below stay inside these ranges and needn't reach their ends.
There are 2 independent parts, one for each index of `groups`. The reference program is written for one: setup_inputs(seed, part) draws one part's arguments, and reference() takes and returns one part's arrays. A program takes and returns all parts, laid end to end along the dimension named above; each array names one. Nothing has to cross between parts.
Inputs may be any that keep to these rules, and one draw needn't show every extreme that they name: `prefill_prefixes`: the lengths sum to 16384 and the largest is exactly 6144; side 0's cache rows hold the prefill transcripts' prefixes one after another in order. `decode_prefixes`: the lengths sum to 16384 and the largest is exactly 8192; side 1's cache rows hold the decode transcripts' prefixes one after another in order. `prefill_counts`: the counts sum to 64 and the largest is exactly 32; side 0's query rows hold the turns in transcript order.
All inputs are finite; a program needn't handle non-finite values.
Results may differ from the reference program's by a relative error of at most 0.0039.
Values may be sent and summed in bfloat16 or wider, within the bound.
A program may use at most 128 MiB of HBM per device.

```python
import math
import jax
import jax.numpy as jnp
import numpy as np
from jax import lax

HEADS = 128
KV_HEADS = 8
HEAD_DIM = 128
QUERY_ROWS = 64
PRE_SEQS = 4
GROUP_SIZE = 16
DEC_SEQS = 32
TURN_MOST = 32
CACHE_ROWS = 16384
PRE_MOST = 6144
DEC_MOST = 8192


def shared_bases(key):
    query_base = jax.random.normal(jax.random.fold_in(key, 501), (2, QUERY_ROWS, HEADS * HEAD_DIM), jnp.float32)
    key_base = jax.random.normal(jax.random.fold_in(key, 502), (2, QUERY_ROWS, KV_HEADS * HEAD_DIM), jnp.float32)
    return (jnp.clip(query_base, -6.0, 6.0), jnp.clip(key_base, -6.0, 6.0))


def draw_fresh_keys(key, part):
    query_base, key_base = shared_bases(key)
    drawn = key_base
    return drawn.astype(jnp.bfloat16)


def draw_queries(key, part):
    query_base, key_base = shared_bases(key)
    drawn = query_base
    return drawn.astype(jnp.bfloat16)


def levels(key, extent, pieces, low, top_value):
    def one(dim, blocks):
        draws = jax.random.uniform(jax.random.fold_in(jax.random.fold_in(key, 6), dim), (blocks,), jnp.float32, low / len(pieces), top_value / len(pieces))
        return jnp.repeat(jnp.exp(draws), extent[dim] // blocks).reshape((-1,) + (1,) * (len(extent) - dim - 1))

    gain = one(*pieces[0])
    for cut in pieces[1:]:
        gain = gain * one(*cut)
    return gain


def profile(count, total, reach, skew):
    weights = [(1 << 20) // math.isqrt(standing ** skew) + 1 for standing in range(2, count + 1)]
    rest, given = total - reach - (count - 1), [1] * (count - 1)
    while rest > 0:
        free = [i for i in range(count - 1) if given[i] < reach]
        pool, left = sum([weights[i] for i in free]), rest
        for i in free:
            more = min(reach - given[i], max(1, left * weights[i] // pool), rest)
            given[i] = given[i] + more
            rest = rest - more
    return np.array([reach] + given)


def uneven_parts(rng, number_of, total, limit, skew):
    if number_of == 2:
        one = jax.random.randint(rng, (), max(1, total - limit), min(limit, total - 1) + 1)
        return jnp.stack([one, total - one])
    tallies = jnp.asarray(profile(number_of, total, limit, skew), jnp.int32)
    pairs = (number_of - 1) // 2
    giver, receiver = tallies[1:1 + 2 * pairs:2], tallies[2:2 + 2 * pairs:2]
    slack = jnp.minimum(giver - 1, limit - receiver)
    moved = jax.random.randint(jax.random.fold_in(rng, 1), (pairs,), 0, 1 << 20) % (slack + 1)
    tallies = tallies.at[1:1 + 2 * pairs:2].set(giver - moved).at[2:2 + 2 * pairs:2].set(receiver + moved)
    return tallies[jax.random.permutation(jax.random.fold_in(rng, 2), number_of)]


def scatter_about(stream_key, extent, scale, bound, pieces=(), kind=jnp.bfloat16):
    result = scale * jax.random.normal(stream_key, extent, jnp.float32)
    if pieces:
        result = result * levels(stream_key, extent, pieces, -0.22, 0.18)
    return jnp.clip(result, -bound, bound).astype(kind)


def setup_inputs(seed: int = 0, part: int = 0) -> dict:
    key_of = jax.random.split(jax.random.key(seed), 9)
    part_keys = jax.random.split(jax.random.fold_in(key_of[8], part), 9)
    queries = draw_queries(jax.random.fold_in(jax.random.fold_in(key_of[8], part), 71), part)
    cache_keys = scatter_about(part_keys[1], (2, CACHE_ROWS, KV_HEADS * HEAD_DIM), 1.0, 6.0, ((1, 16),))
    cache_values = scatter_about(part_keys[2], (2, CACHE_ROWS, KV_HEADS * HEAD_DIM), 1.0, 6.0, ((1, 16),))
    fresh_keys = draw_fresh_keys(jax.random.fold_in(jax.random.fold_in(key_of[8], part), 71), part)
    fresh_values = scatter_about(part_keys[4], (2, QUERY_ROWS, KV_HEADS * HEAD_DIM), 1.0, 6.0, ((2, 16),))
    prefill_prefixes = uneven_parts(part_keys[5], PRE_SEQS, CACHE_ROWS, PRE_MOST, 2).astype(jnp.int32)
    decode_prefixes = uneven_parts(part_keys[6], DEC_SEQS, CACHE_ROWS, DEC_MOST, 2).astype(jnp.int32)
    prefill_counts = uneven_parts(part_keys[7], PRE_SEQS, QUERY_ROWS, TURN_MOST, 2).astype(jnp.int32)
    return dict(queries=queries, cache_keys=cache_keys, cache_values=cache_values, fresh_keys=fresh_keys, fresh_values=fresh_values, prefill_prefixes=prefill_prefixes, decode_prefixes=decode_prefixes, prefill_counts=prefill_counts)


def owner_of(counts, length):
    ends = jnp.cumsum(counts).astype(jnp.int32)
    places = jnp.arange(length, dtype=jnp.int32)
    return jnp.sum((places[:, None] >= ends[None, :]).astype(jnp.int32), axis=1)


def one_side(queries, cache_keys, cache_values, fresh_keys, fresh_values, prefix_lengths, query_counts):
    query_rows = queries.shape[0]
    query_owner = owner_of(query_counts, query_rows)
    cache_owner = owner_of(prefix_lengths, cache_keys.shape[0])
    places = jnp.arange(query_rows, dtype=jnp.int32)
    cache_visible = query_owner[:, None] == cache_owner[None, :]
    turn_visible = (query_owner[:, None] == query_owner[None, :]) & (places[None, :] <= places[:, None])
    visible = jnp.concatenate([cache_visible, turn_visible], axis=1)
    all_keys = jnp.concatenate([cache_keys, fresh_keys], axis=0).astype(jnp.float32)
    all_keys = all_keys.reshape(-1, KV_HEADS, HEAD_DIM).transpose(1, 0, 2)
    all_values = jnp.concatenate([cache_values, fresh_values], axis=0).astype(jnp.float32)
    all_values = all_values.reshape(-1, KV_HEADS, HEAD_DIM).transpose(1, 0, 2)
    grouped = queries.astype(jnp.float32).reshape(query_rows, KV_HEADS, GROUP_SIZE, HEAD_DIM).transpose(1, 2, 0, 3)

    def per_group(operands):
        group_queries, group_keys, group_values = operands
        scores = jnp.einsum("aqd,kd->aqk", group_queries, group_keys) * (HEAD_DIM ** -0.5)
        scores = jnp.where(visible[None], scores, -1e30)
        row_max = jnp.max(scores, axis=2, keepdims=True)
        weights = jnp.exp(scores - row_max)
        denominator = jnp.sum(weights, axis=2)
        rounded = lax.optimization_barrier(weights.astype(jnp.bfloat16)).astype(jnp.float32)
        numerator = jnp.einsum("aqk,kd->qad", rounded, group_values)
        return numerator / denominator.T[:, :, None]

    mixed = lax.map(per_group, (grouped, all_keys, all_values))
    return mixed.transpose(1, 0, 2, 3).reshape(query_rows, HEADS * HEAD_DIM).astype(jnp.bfloat16)


def reference(queries, cache_keys, cache_values, fresh_keys, fresh_values, prefill_prefixes, decode_prefixes, prefill_counts):
    decode_counts = jnp.full((DEC_SEQS,), 2, jnp.int32)
    prefill_side = one_side(queries[0], cache_keys[0], cache_values[0], fresh_keys[0], fresh_values[0],
                            prefill_prefixes, prefill_counts)
    decode_side = one_side(queries[1], cache_keys[1], cache_values[1], fresh_keys[1], fresh_values[1],
                           decode_prefixes, decode_counts)
    attended = jnp.stack([prefill_side, decode_side])
    handed_keys = jnp.stack([fresh_keys[1], fresh_keys[0]])
    handed_values = jnp.stack([fresh_values[1], fresh_values[0]])
    return (attended, handed_keys, handed_values)
```

```python
import jax
import jax.numpy as jnp
from jax import lax
from jax.experimental import pallas as pl
from jax.experimental.pallas import tpu as pltpu
from jax.sharding import PartitionSpec as P

HEADS = 128
KV_HEADS = 8
HEAD_DIM = 128
GROUP_SIZE = 16


def passed_along(block, axis, distance):
    devices = range(lax.axis_size(axis))
    route = [((i - distance) % len(devices), i) for i in devices]
    return lax.ppermute(block, axis, route)


def owner_range(counts, start, length):
    ends = jnp.cumsum(counts)
    places = start + jnp.arange(length, dtype=jnp.int32)
    return jnp.sum((places[:, None] >= ends[None, :]).astype(jnp.int32), axis=1)


def masked_scores(grouped, key_block, visible):
    scores = jnp.einsum("qgad,kgd->gaqk", grouped, key_block, preferred_element_type=jnp.float32)
    scores = scores * HEAD_DIM ** (-0.5)
    return jnp.where(visible[None, None], scores, -1e30)


def shards(
    queries,
    cache_keys,
    cache_values,
    fresh_keys,
    fresh_values,
    prefill_prefixes,
    decode_prefixes,
    prefill_counts,
):
    device_place = lax.axis_index("tp")
    device_count = lax.axis_size("tp")
    side_place = lax.axis_index("role")
    local_sides = queries.shape[0]
    gathered = lax.all_gather(queries, "tp", axis=2, tiled=True)
    query_rows = gathered.shape[1]
    turn_keys, turn_values = (
        lax.all_to_all(fresh_keys, "tp", split_axis=1, concat_axis=2, tiled=True),
        lax.all_to_all(fresh_values, "tp", split_axis=1, concat_axis=2, tiled=True),
    )
    shifted_keys, shifted_values = passed_along((turn_keys, turn_values), "role", 1)
    handed_keys = jnp.flip(shifted_keys, axis=0)
    handed_values = jnp.flip(shifted_values, axis=0)
    query_places = jnp.arange(query_rows, dtype=jnp.int32)
    cache_rows = cache_keys.shape[1]
    cache_start = device_place * cache_rows
    turn_rows = turn_keys.shape[1]
    turn_places = device_place * turn_rows + jnp.arange(turn_rows, dtype=jnp.int32)
    block_rows = min(512, cache_rows)
    side_blocks = []
    side_grouped = []
    for local in range(local_sides):
        is_prefill = side_place * local_sides + local == 0
        query_owner = jnp.where(
            is_prefill, owner_range(prefill_counts, 0, query_rows), query_places // 2
        )
        cache_owner = jnp.where(
            is_prefill,
            owner_range(prefill_prefixes, cache_start, cache_rows),
            owner_range(decode_prefixes, cache_start, cache_rows),
        )
        turn_owner = jnp.where(
            is_prefill,
            owner_range(prefill_counts, device_place * turn_rows, turn_rows),
            turn_places // 2,
        )
        turn_visible = (query_owner[:, None] == turn_owner[None, :]) & (
            turn_places[None, :] <= query_places[:, None]
        )
        blocks = []
        for block_start in range(0, cache_rows, block_rows):
            key_block = cache_keys[local, block_start : block_start + block_rows].reshape(
                block_rows, KV_HEADS, HEAD_DIM
            )
            value_block = cache_values[local, block_start : block_start + block_rows].reshape(
                block_rows, KV_HEADS, HEAD_DIM
            )
            visible = (
                query_owner[:, None] == cache_owner[None, block_start : block_start + block_rows]
            )
            blocks.append((key_block, value_block, visible))
        blocks.append(
            (
                turn_keys[local].reshape(turn_rows, KV_HEADS, HEAD_DIM),
                turn_values[local].reshape(turn_rows, KV_HEADS, HEAD_DIM),
                turn_visible,
            )
        )
        side_blocks.append(blocks)
        side_grouped.append(gathered[local].reshape(query_rows, KV_HEADS, GROUP_SIZE, HEAD_DIM))
    maxima = []
    for local in range(local_sides):
        local_max = jnp.full((KV_HEADS, GROUP_SIZE, query_rows), -1e30, jnp.float32)
        for key_block, value_block, visible in side_blocks[local]:
            local_max = jnp.maximum(
                local_max, jnp.max(masked_scores(side_grouped[local], key_block, visible), axis=3)
            )
        maxima.append(local_max)
    row_max_all = lax.pmax(jnp.stack(maxima), "tp")
    numerators = []
    denominators = []
    for local in range(local_sides):
        row_max = row_max_all[local]
        numerator = jnp.zeros((query_rows, KV_HEADS, GROUP_SIZE, HEAD_DIM), jnp.float32)
        denominator = jnp.zeros((KV_HEADS, GROUP_SIZE, query_rows), jnp.float32)
        for key_block, value_block, visible in side_blocks[local]:
            weights = jnp.exp(
                masked_scores(side_grouped[local], key_block, visible) - row_max[..., None]
            )
            denominator = denominator + jnp.sum(weights, axis=3)
            numerator = numerator + jnp.einsum(
                "gaqk,kgd->qgad",
                weights.astype(jnp.bfloat16),
                value_block,
                preferred_element_type=jnp.float32,
            )
        numerators.append(numerator.reshape(query_rows, HEADS * HEAD_DIM))
        denominators.append(denominator.transpose(2, 0, 1).reshape(query_rows, HEADS))
    flat_numerator = jnp.stack(numerators)
    flat_denominator = jnp.stack(denominators)
    summed, totals = lax.psum((flat_numerator, flat_denominator), "tp")
    column_width = summed.shape[2] // device_count
    head_width = totals.shape[2] // device_count
    summed = lax.dynamic_slice_in_dim(summed, device_place * column_width, column_width, 2)
    totals = lax.dynamic_slice_in_dim(totals, device_place * head_width, head_width, 2)
    shares = summed.reshape(local_sides, query_rows, -1, HEAD_DIM) / totals[:, :, :, None]
    attended = shares.reshape(local_sides, query_rows, -1).astype(jnp.bfloat16)
    return (attended, handed_keys, handed_values)

TP = 16
ZS = 4
BLOCK = 512
TILES = 4
HEADS_PER_STEP = 2
SCALE = HEAD_DIM ** (-0.5)
MESH = pl.DeviceIdType.MESH
LIMIT = 48 * 1024 * 1024


def place(z, y, c):
    return (z * 2 + y) * 2 + c


def greet(me):
    barrier = pltpu.get_barrier_semaphore()
    for d in range(1, TP):
        pl.semaphore_signal(
            barrier, inc=1, device_id={"tp": lax.rem(me + d, TP)}, device_id_type=MESH
        )
    pl.semaphore_wait(barrier, TP - 1)


def remote(src, dst, send, recv, to):
    return pltpu.make_async_remote_copy(
        src_ref=src, dst_ref=dst, send_sem=send, recv_sem=recv,
        device_id={"tp": to}, device_id_type=MESH,
    )


def gather_kernel(q_ref, f_ref, out_ref, fout_ref, send, recv, fsend, frecv, local):
    me = lax.axis_index("tp")
    c, y, z = lax.rem(me, 2), lax.rem(me // 2, 2), me // 4
    other_y, other_c = place(z, 1 - y, c), place(z, y, 1 - c)
    greet(me)
    own = [
        pltpu.make_async_copy(q_ref, out_ref.at[me], local.at[0]),
        pltpu.make_async_copy(f_ref.at[me], fout_ref.at[me], local.at[1]),
    ]
    for copy in own:
        copy.start()
    sends = []

    def push(src, origin, s, to):
        copy = remote(
            src, out_ref.at[origin, s], send.at[len(sends)], recv.at[origin * 2 + s], to
        )
        copy.start()
        sends.append(copy)

    def arrived(origin, s):
        remote(
            out_ref.at[origin, s], out_ref.at[origin, s], send.at[0],
            recv.at[origin * 2 + s], other_c,
        ).wait_recv()

    for s in range(2):
        for dz in (2, 1, 3):
            push(q_ref.at[s], me, s, place(lax.rem(z + dz, ZS), y, c))
        push(q_ref.at[s], me, s, other_y)
        push(q_ref.at[s], me, s, other_c)
    fresh = []
    for d in range(1, TP):
        to = lax.rem(me + d, TP)
        copy = remote(f_ref.at[to], fout_ref.at[me], fsend.at[d], frecv.at[d], to)
        copy.start()
        fresh.append(copy)
    for s in range(2):
        for dz in (1, 3, 2):
            origin = place(lax.rem(z + dz, ZS), y, c)
            arrived(origin, s)
            push(out_ref.at[origin, s], origin, s, other_y)
            push(out_ref.at[origin, s], origin, s, other_c)
    for s in range(2):
        for dz in (0, 1, 3, 2):
            origin = place(lax.rem(z + dz, ZS), 1 - y, c)
            arrived(origin, s)
            push(out_ref.at[origin, s], origin, s, other_c)
    for s in range(2):
        for row in range(2):
            for dz in range(ZS):
                arrived(place(lax.rem(z + dz, ZS), row, 1 - c), s)
    for d in range(1, TP):
        src = lax.rem(me - d + TP, TP)
        remote(f_ref.at[src], fout_ref.at[src], fsend.at[d], frecv.at[d], src).wait_recv()
    for copy in sends + fresh:
        copy.wait_send()
    for copy in own:
        copy.wait()


def max_kernel(m_ref, out_ref, slots, send, recv, send2, recv2):
    me = lax.axis_index("tp")
    greet(me)
    first, second = [], []
    for d in range(1, TP):
        to = lax.rem(me + d, TP)
        copy = remote(m_ref.at[to], slots.at[d - 1], send.at[d], recv.at[d], to)
        copy.start()
        first.append(copy)
    best = m_ref[me]
    for d in range(1, TP):
        first[d - 1].wait_recv()
        best = jnp.maximum(best, slots[d - 1])
    out_ref[me] = best
    for d in range(1, TP):
        to = lax.rem(me + d, TP)
        copy = remote(out_ref.at[me], out_ref.at[me], send2.at[d], recv2.at[d], to)
        copy.start()
        second.append(copy)
    for d in range(1, TP):
        src = lax.rem(me - d + TP, TP)
        remote(
            out_ref.at[src], out_ref.at[src], send2.at[d], recv2.at[d], src
        ).wait_recv()
    for copy in first + second:
        copy.wait_send()


def reduce_kernel(
    num_ref, l_ref, out_ref, c_in, y_out, y_in, z_out, z_in, l_in,
    c_send, c_recv, y_send, y_recv, z_send, z_recv, l_send, l_recv,
):
    me = lax.axis_index("tp")
    c, y, z = lax.rem(me, 2), lax.rem(me // 2, 2), me // 4
    other_y, other_c = place(z, 1 - y, c), place(z, y, 1 - c)
    greet(me)
    c_copies, y_copies, z_copies, l_copies = {}, {}, {}, []
    for s in range(2):
        for near in range(2):
            row = y if near else 1 - y
            for dz in range(ZS):
                to_z = lax.rem(z + dz, ZS)
                at = (s * 2 + near) * ZS + dz
                copy = remote(
                    num_ref.at[place(to_z, row, 1 - c), s], c_in.at[at],
                    c_send.at[at], c_recv.at[at], other_c,
                )
                copy.start()
                c_copies[at] = copy
    for d in range(1, TP):
        to = lax.rem(me + d, TP)
        copy = remote(l_ref.at[to], l_in.at[d - 1], l_send.at[d], l_recv.at[d], to)
        copy.start()
        l_copies.append(copy)
    order = (2, 1, 3, 0)
    for s in range(2):
        for dz in order:
            at, slot = s * 2 * ZS + dz, s * ZS + dz
            c_copies[at].wait_recv()
            dest = place(lax.rem(z + dz, ZS), 1 - y, c)
            y_out[slot] = (num_ref[dest, s] + c_in[at]).astype(jnp.bfloat16)
            copy = remote(
                y_out.at[slot], y_in.at[slot], y_send.at[slot], y_recv.at[slot], other_y
            )
            copy.start()
            y_copies[slot] = copy
    kept = []
    for s in range(2):
        for dz in order:
            at, slot = (s * 2 + 1) * ZS + dz, s * ZS + dz
            c_copies[at].wait_recv()
            y_copies[slot].wait_recv()
            to = place(lax.rem(z + dz, ZS), y, c)
            total = num_ref[to, s] + c_in[at] + y_in[slot].astype(jnp.float32)
            if dz == 0:
                c_in[at] = total
            else:
                z_out[slot] = total.astype(jnp.bfloat16)
                copy = remote(
                    z_out.at[slot], z_in.at[slot], z_send.at[slot], z_recv.at[slot], to
                )
                copy.start()
                z_copies[slot] = copy
    totals = l_ref[me]
    for d in range(1, TP):
        l_copies[d - 1].wait_recv()
        totals = totals + l_in[d - 1]
    columns = totals.T
    for s in range(2):
        for dz in (1, 3, 2):
            z_copies[s * ZS + dz].wait_recv()
        for j in range(TILES):
            rows = slice(128 * j, 128 * j + 128)
            total = c_in[(s * 2 + 1) * ZS, rows]
            for dz in range(1, ZS):
                total = total + z_in[s * ZS + dz, rows].astype(jnp.float32)
            at = s * TILES + j
            out_ref[s, rows] = (total / columns[:, at : at + 1]).astype(jnp.bfloat16)
    for copy in [*c_copies.values(), *y_copies.values(), *z_copies.values(), *l_copies]:
        copy.wait_send()


def scores_of(q_ref, k_ref, bound_ref, h, j, kind, block):
    q = q_ref[h, :, 0, 128 * j : 128 * j + 128, :].reshape(256, HEAD_DIM)
    rows = BLOCK if kind == 0 else k_ref.shape[1]
    k = k_ref[0, rows * block : rows * block + rows, HEAD_DIM * h : HEAD_DIM * h + HEAD_DIM]
    s = lax.dot_general(
        k, q, (((1,), (1,)), ((), ())), preferred_element_type=jnp.float32
    )
    at = lax.broadcasted_iota(jnp.int32, s.shape, 0)
    low = bound_ref[0, j, 2 * kind : 2 * kind + 1, :] - rows * block
    high = bound_ref[0, j, 2 * kind + 1 : 2 * kind + 2, :] - rows * block
    return jnp.where((at >= low) & (at < high), s, -1e30)


def pieces(k_ref):
    count = k_ref.shape[1] // BLOCK
    return [(0, b) for b in range(count)] + [(1, 0)]


def local_max_kernel(flag_ref, q_ref, k_ref, t_ref, bound_ref, m_ref):
    side = pl.program_id(0)
    m_ref[...] = jnp.full(m_ref.shape, -1e30, jnp.float32)
    parts = pieces(k_ref)
    for j in range(TILES):
        for n, (kind, block) in enumerate(parts):
            @pl.when(flag_ref[(side * len(parts) + n) * TILES + j] != 0)
            def _():
                for h in range(HEADS_PER_STEP):
                    s = scores_of(q_ref, t_ref if kind else k_ref, bound_ref, h, j, kind, block)
                    top = jnp.max(s, axis=0, keepdims=True)
                    for p in range(2):
                        row = m_ref[h, p, 0, j : j + 1, :]
                        m_ref[h, p, 0, j : j + 1, :] = jnp.maximum(
                            row, top[:, 128 * p : 128 * p + 128]
                        )


def weigh_kernel(
    flag_ref, q_ref, k_ref, v_ref, t_ref, u_ref, bound_ref, m_ref, num_ref, l_ref, total
):
    side = pl.program_id(0)
    l_ref[...] = jnp.zeros(l_ref.shape, jnp.float32)
    parts = pieces(k_ref)
    for j in range(TILES):
        total[...] = jnp.zeros_like(total)
        for n, (kind, block) in enumerate(parts):
            @pl.when(flag_ref[(side * len(parts) + n) * TILES + j] != 0)
            def _():
                for h in range(HEADS_PER_STEP):
                    s = scores_of(q_ref, t_ref if kind else k_ref, bound_ref, h, j, kind, block)
                    top = jnp.concatenate(
                        [m_ref[h, p, 0, j : j + 1, :] for p in range(2)], axis=1
                    )
                    w = jnp.exp((s - top) * SCALE)
                    sums = jnp.sum(w, axis=0, keepdims=True)
                    for p in range(2):
                        l_ref[h, p, 0, j : j + 1, :] += sums[:, 128 * p : 128 * p + 128]
                    rows = s.shape[0]
                    v = (u_ref if kind else v_ref)[
                        0, rows * block : rows * block + rows,
                        HEAD_DIM * h : HEAD_DIM * h + HEAD_DIM,
                    ]
                    total[h] += lax.dot_general(
                        v, w.astype(jnp.bfloat16), (((0,), (0,)), ((), ())),
                        preferred_element_type=jnp.float32,
                    )
        for h in range(HEADS_PER_STEP):
            done = total[h].T
            for p in range(2):
                num_ref[h, p, 0, 128 * j : 128 * j + 128, :] = done[128 * p : 128 * p + 128]


def spans(counts, owner):
    t = jnp.arange(counts.shape[0], dtype=jnp.int32)
    start = jnp.sum(jnp.where(t[None] < owner[:, None], counts[None], 0), axis=1)
    return start, start + jnp.sum(jnp.where(t[None] == owner[:, None], counts[None], 0), axis=1)


def fast_shards(
    queries,
    cache_keys,
    cache_values,
    fresh_keys,
    fresh_values,
    prefill_prefixes,
    decode_prefixes,
    prefill_counts,
):
    me = lax.axis_index("tp")
    query_rows = queries.shape[1]
    cache_rows = cache_keys.shape[1]
    turn_rows = query_rows // TP
    q = queries.reshape(2, query_rows * 8, HEAD_DIM)
    fresh = jnp.stack([fresh_keys, fresh_values]).reshape(2, 2, TP, turn_rows, -1)
    fresh = fresh.transpose(2, 0, 1, 3, 4).reshape(TP, 4 * turn_rows, -1)
    fresh = jnp.pad(fresh, ((0, 0), (0, 0), (0, 64)))
    any_spec = pl.BlockSpec(memory_space=pl.ANY)
    vmem_spec = pl.BlockSpec(memory_space=pltpu.VMEM)
    dma = pltpu.SemaphoreType.DMA
    gathered, turns = pl.pallas_call(
        gather_kernel,
        out_shape=(
            jax.ShapeDtypeStruct((TP, *q.shape), jnp.bfloat16),
            jax.ShapeDtypeStruct(fresh.shape, jnp.bfloat16),
        ),
        in_specs=[any_spec] * 2,
        out_specs=(any_spec, any_spec),
        scratch_shapes=[dma((32,)), dma((32,)), dma((TP,)), dma((TP,)), dma((2,))],
        compiler_params=pltpu.CompilerParams(collective_id=0, has_side_effects=True),
        name="gather_queries",
    )(q, fresh)
    turns = turns[:, :, :64].reshape(TP, 2, 2, turn_rows, 64)
    turns = turns.transpose(1, 2, 3, 0, 4).reshape(2, 2, turn_rows, -1)
    handed_keys, handed_values = jnp.flip(turns[0], axis=0), jnp.flip(turns[1], axis=0)
    padded = jnp.pad(turns, ((0, 0), (0, 0), (0, 16 - turn_rows), (0, 0)))

    places = jnp.arange(query_rows, dtype=jnp.int32)
    t = jnp.arange(prefill_counts.shape[0], dtype=jnp.int32)
    ends = jnp.sum(jnp.where(t[None] <= t[:, None], prefill_counts[None], 0), axis=1)
    owner = jnp.sum((places[:, None] >= ends[None]).astype(jnp.int32), axis=1)
    turn_start = spans(prefill_counts, owner)[0]
    start, end = zip(spans(prefill_prefixes, owner), spans(decode_prefixes, places // 2))
    cache_start, cache_end = jnp.stack(start), jnp.stack(end)
    turn_start = jnp.stack([turn_start, places // 2 * 2])
    turn_end = jnp.broadcast_to(places + 1, (2, query_rows))
    cache_start, cache_end = cache_start - me * cache_rows, cache_end - me * cache_rows
    turn_start = turn_start - me * turn_rows
    turn_end = jnp.minimum(turn_end - me * turn_rows, turn_rows)
    bounds = jnp.stack([cache_start, cache_end, turn_start, turn_end], axis=1)
    tiled = bounds.reshape(2, 4, TILES, query_rows // TILES).transpose(0, 2, 1, 3)
    wide = jnp.broadcast_to(
        tiled[:, :, :, None, :, None], (2, TILES, 4, 2, query_rows // TILES, 8)
    ).reshape(2, TILES, 4, 256)
    flags = []
    for b in range(cache_rows // BLOCK):
        flags.append((tiled[:, :, 0] < (b + 1) * BLOCK) & (tiled[:, :, 1] > b * BLOCK))
    flags.append((tiled[:, :, 2] < tiled[:, :, 3]) & (tiled[:, :, 3] > 0))
    flags = jnp.any(jnp.stack(flags, axis=1), axis=-1).astype(jnp.int32).reshape(-1)

    hs = HEADS_PER_STEP
    smem = pl.BlockSpec(memory_space=pltpu.SMEM)
    q_spec = pl.BlockSpec((hs, 2, 1, 512, HEAD_DIM), lambda s, g: (g, 0, s, 0, 0))
    n_spec = pl.BlockSpec((hs, 2, 1, 512, HEAD_DIM), lambda s, g: (g, 0, s, 0, 0))
    k_spec = pl.BlockSpec((1, cache_rows, hs * HEAD_DIM), lambda s, g: (s, 0, g))
    t_spec = pl.BlockSpec((1, 16, hs * HEAD_DIM), lambda s, g: (s, 0, g))
    b_spec = pl.BlockSpec((1, TILES, 4, 256), lambda s, g: (s, 0, 0, 0))
    m_spec = pl.BlockSpec((hs, 2, 1, TILES, 128), lambda s, g: (g, 0, s, 0, 0))
    stats = jax.ShapeDtypeStruct((KV_HEADS, 2, 2, TILES, 128), jnp.float32)
    grid = (2, KV_HEADS // hs)
    params = pltpu.CompilerParams(vmem_limit_bytes=LIMIT)
    gathered = gathered.reshape(KV_HEADS, 2, *q.shape)
    local_max = pl.pallas_call(
        local_max_kernel,
        grid=grid,
        out_shape=stats,
        in_specs=[smem, q_spec, k_spec, t_spec, b_spec],
        out_specs=m_spec,
        compiler_params=params,
        name="local_max",
    )(flags, gathered, cache_keys, padded[0], wide)
    row_max = pl.pallas_call(
        max_kernel,
        out_shape=jax.ShapeDtypeStruct((TP, 8, 128), jnp.float32),
        in_specs=[vmem_spec],
        out_specs=vmem_spec,
        scratch_shapes=[pltpu.VMEM((TP - 1, 8, 128), jnp.float32)] + [dma((TP,))] * 4,
        compiler_params=pltpu.CompilerParams(collective_id=1, has_side_effects=True),
        name="row_max",
    )(local_max.reshape(TP, 8, 128))
    numerator, denominator = pl.pallas_call(
        weigh_kernel,
        grid=grid,
        out_shape=(
            jax.ShapeDtypeStruct((KV_HEADS, 2, 2, 512, HEAD_DIM), jnp.float32), stats,
        ),
        in_specs=[smem, q_spec, k_spec, k_spec, t_spec, t_spec, b_spec, m_spec],
        out_specs=(n_spec, m_spec),
        scratch_shapes=[pltpu.VMEM((hs, HEAD_DIM, 256), jnp.float32)],
        compiler_params=params,
        name="weigh_values",
    )(
        flags, gathered, cache_keys, cache_values, padded[0], padded[1], wide,
        row_max.reshape(stats.shape),
    )
    piece = (512, HEAD_DIM)
    attended = pl.pallas_call(
        reduce_kernel,
        out_shape=jax.ShapeDtypeStruct((2, *piece), jnp.bfloat16),
        in_specs=[vmem_spec] * 2,
        out_specs=vmem_spec,
        scratch_shapes=[
            pltpu.VMEM((16, *piece), jnp.float32),
            pltpu.VMEM((8, *piece), jnp.bfloat16),
            pltpu.VMEM((8, *piece), jnp.bfloat16),
            pltpu.VMEM((8, *piece), jnp.bfloat16),
            pltpu.VMEM((8, *piece), jnp.bfloat16),
            pltpu.VMEM((TP - 1, 8, 128), jnp.float32),
            dma((16,)), dma((16,)), dma((8,)), dma((8,)), dma((8,)), dma((8,)),
            dma((TP,)), dma((TP,)),
        ],
        compiler_params=pltpu.CompilerParams(
            collective_id=2, has_side_effects=True, vmem_limit_bytes=LIMIT
        ),
        name="reduce_numerators",
    )(numerator.reshape(TP, 2, *piece), denominator.reshape(TP, 8, 128))
    return attended.reshape(queries.shape), handed_keys, handed_values


def solution(mesh):
    fast = mesh.shape["tp"] == TP and mesh.shape["role"] == 1
    return jax.shard_map(
        fast_shards if fast else shards,
        mesh=mesh,
        in_specs=(
            P(("groups", "role"), None, "tp"),
            P(("groups", "role"), "tp", None),
            P(("groups", "role"), "tp", None),
            P(("groups", "role"), None, "tp"),
            P(("groups", "role"), None, "tp"),
            P("groups"),
            P("groups"),
            P("groups"),
        ),
        out_specs=(
            P(("groups", "role"), None, "tp"),
            P(("groups", "role"), "tp", None),
            P(("groups", "role"), "tp", None),
        ),
        check_vma=False,
    )
```

```python
import math

import jax
import jax.numpy as jnp
from jax import lax
from jax.experimental import pallas as pl
from jax.experimental.pallas import tpu as pltpu
from jax.sharding import PartitionSpec as P

HEADS = 128
KV_HEADS = 8
HEAD_DIM = 128
GROUP_SIZE = 16


def passed_along(block, axis, distance):
    devices = range(lax.axis_size(axis))
    route = [((i - distance) % len(devices), i) for i in devices]
    return lax.ppermute(block, axis, route)


def owner_range(counts, start, length):
    ends = jnp.cumsum(counts)
    places = start + jnp.arange(length, dtype=jnp.int32)
    return jnp.sum((places[:, None] >= ends[None, :]).astype(jnp.int32), axis=1)


def masked_scores(grouped, key_block, visible):
    scores = jnp.einsum("qgad,kgd->gaqk", grouped, key_block, preferred_element_type=jnp.float32)
    scores = scores * HEAD_DIM ** (-0.5)
    return jnp.where(visible[None, None], scores, -1e30)


def shards(
    queries,
    cache_keys,
    cache_values,
    fresh_keys,
    fresh_values,
    prefill_prefixes,
    decode_prefixes,
    prefill_counts,
):
    device_place = lax.axis_index("tp")
    device_count = lax.axis_size("tp")
    side_place = lax.axis_index("role")
    local_sides = queries.shape[0]
    gathered = lax.all_gather(queries, "tp", axis=2, tiled=True)
    query_rows = gathered.shape[1]
    turn_keys, turn_values = (
        lax.all_to_all(fresh_keys, "tp", split_axis=1, concat_axis=2, tiled=True),
        lax.all_to_all(fresh_values, "tp", split_axis=1, concat_axis=2, tiled=True),
    )
    shifted_keys, shifted_values = passed_along((turn_keys, turn_values), "role", 1)
    handed_keys = jnp.flip(shifted_keys, axis=0)
    handed_values = jnp.flip(shifted_values, axis=0)
    query_places = jnp.arange(query_rows, dtype=jnp.int32)
    cache_rows = cache_keys.shape[1]
    cache_start = device_place * cache_rows
    turn_rows = turn_keys.shape[1]
    turn_places = device_place * turn_rows + jnp.arange(turn_rows, dtype=jnp.int32)
    block_rows = min(512, cache_rows)
    side_blocks = []
    side_grouped = []
    for local in range(local_sides):
        is_prefill = side_place * local_sides + local == 0
        query_owner = jnp.where(
            is_prefill, owner_range(prefill_counts, 0, query_rows), query_places // 2
        )
        cache_owner = jnp.where(
            is_prefill,
            owner_range(prefill_prefixes, cache_start, cache_rows),
            owner_range(decode_prefixes, cache_start, cache_rows),
        )
        turn_owner = jnp.where(
            is_prefill,
            owner_range(prefill_counts, device_place * turn_rows, turn_rows),
            turn_places // 2,
        )
        turn_visible = (query_owner[:, None] == turn_owner[None, :]) & (
            turn_places[None, :] <= query_places[:, None]
        )
        blocks = []
        for block_start in range(0, cache_rows, block_rows):
            key_block = cache_keys[local, block_start : block_start + block_rows].reshape(
                block_rows, KV_HEADS, HEAD_DIM
            )
            value_block = cache_values[local, block_start : block_start + block_rows].reshape(
                block_rows, KV_HEADS, HEAD_DIM
            )
            visible = (
                query_owner[:, None] == cache_owner[None, block_start : block_start + block_rows]
            )
            blocks.append((key_block, value_block, visible))
        blocks.append(
            (
                turn_keys[local].reshape(turn_rows, KV_HEADS, HEAD_DIM),
                turn_values[local].reshape(turn_rows, KV_HEADS, HEAD_DIM),
                turn_visible,
            )
        )
        side_blocks.append(blocks)
        side_grouped.append(gathered[local].reshape(query_rows, KV_HEADS, GROUP_SIZE, HEAD_DIM))
    maxima = []
    for local in range(local_sides):
        local_max = jnp.full((KV_HEADS, GROUP_SIZE, query_rows), -1e30, jnp.float32)
        for key_block, value_block, visible in side_blocks[local]:
            local_max = jnp.maximum(
                local_max, jnp.max(masked_scores(side_grouped[local], key_block, visible), axis=3)
            )
        maxima.append(local_max)
    row_max_all = lax.pmax(jnp.stack(maxima), "tp")
    numerators = []
    denominators = []
    for local in range(local_sides):
        row_max = row_max_all[local]
        numerator = jnp.zeros((query_rows, KV_HEADS, GROUP_SIZE, HEAD_DIM), jnp.float32)
        denominator = jnp.zeros((KV_HEADS, GROUP_SIZE, query_rows), jnp.float32)
        for key_block, value_block, visible in side_blocks[local]:
            weights = jnp.exp(
                masked_scores(side_grouped[local], key_block, visible) - row_max[..., None]
            )
            denominator = denominator + jnp.sum(weights, axis=3)
            numerator = numerator + jnp.einsum(
                "gaqk,kgd->qgad",
                weights.astype(jnp.bfloat16),
                value_block,
                preferred_element_type=jnp.float32,
            )
        numerators.append(numerator.reshape(query_rows, HEADS * HEAD_DIM))
        denominators.append(denominator.transpose(2, 0, 1).reshape(query_rows, HEADS))
    flat_numerator = jnp.stack(numerators)
    flat_denominator = jnp.stack(denominators)
    summed, totals = lax.psum((flat_numerator, flat_denominator), "tp")
    column_width = summed.shape[2] // device_count
    head_width = totals.shape[2] // device_count
    summed = lax.dynamic_slice_in_dim(summed, device_place * column_width, column_width, 2)
    totals = lax.dynamic_slice_in_dim(totals, device_place * head_width, head_width, 2)
    shares = summed.reshape(local_sides, query_rows, -1, HEAD_DIM) / totals[:, :, :, None]
    attended = shares.reshape(local_sides, query_rows, -1).astype(jnp.bfloat16)
    return (attended, handed_keys, handed_values)

TP = 16
ZS = 4
HALF = 256
WIDTH = 8 * 64
TURN_PAD = 16
SCALE = HEAD_DIM ** (-0.5) * math.log2(math.e)
MESH = pl.DeviceIdType.MESH
LIMIT = 56 * 1024 * 1024


def place(z, y, c):
    return (z * 2 + y) * 2 + c


def greet(me):
    barrier = pltpu.get_barrier_semaphore()
    for d in range(1, TP):
        pl.semaphore_signal(
            barrier, inc=1, device_id={"tp": lax.rem(me + d, TP)}, device_id_type=MESH
        )
    pl.semaphore_wait(barrier, TP - 1)


def remote(src, dst, send, recv, to):
    return pltpu.make_async_remote_copy(
        src_ref=src, dst_ref=dst, send_sem=send, recv_sem=recv,
        device_id={"tp": to}, device_id_type=MESH,
    )


def each(count, body):
    def step(i, carry):
        body(i)
        return carry

    lax.fori_loop(0, count, step, 0)


def cache_copy(cache_ref, rows_ref, sem, s, h):
    columns = pl.ds(pl.multiple_of(h * HEAD_DIM, HEAD_DIM), HEAD_DIM)
    count = cache_ref.shape[1]
    return pltpu.make_async_copy(
        cache_ref.at[s, :, columns], rows_ref.at[s, h, pl.ds(0, count), :], sem.at[s * KV_HEADS + h]
    )


def place_turns(turn_ref, rows_ref, values):
    count = rows_ref.shape[2] - TURN_PAD

    def body(h):
        rows = turn_ref[2 * h].astype(jnp.float32) + turn_ref[2 * h + 1].astype(jnp.float32)
        if values:
            rows = jnp.concatenate([rows[8:], rows[:8]], axis=0)
        for s in range(2):
            rows_ref[s, h, count:, :] = rows.astype(jnp.bfloat16)

    each(KV_HEADS, body)


def masked(q_ref, qa_ref, k_ref, ka_ref, origin, s, h, part):
    rows = slice(HALF * part, HALF * part + HALF)
    q = jnp.concatenate([q_ref[origin, s, rows, :], qa_ref[s, rows, :]], axis=1)
    k = jnp.concatenate([k_ref[s, h], ka_ref[s]], axis=1)
    return lax.dot_general(
        k, q, (((1,), (1,)), ((), ())), preferred_element_type=jnp.float32
    )


def gather_kernel(
    q_ref, f_ref, keys_ref, ka_ref, qa_ref, out_ref, turn_ref, max_ref,
    rows, local_max, slots,
    send, recv, fsend, frecv, local, loads, msend, mrecv, gsend, grecv,
):
    me = lax.axis_index("tp")
    c, y, z = lax.rem(me, 2), lax.rem(me // 2, 2), me // 4
    other_y, other_c = place(z, 1 - y, c), place(z, y, 1 - c)
    for s in range(2):
        each(KV_HEADS, lambda h: cache_copy(keys_ref, rows, loads, s, h).start())
    greet(me)
    own = [
        pltpu.make_async_copy(q_ref, out_ref.at[me], local.at[0]),
        pltpu.make_async_copy(f_ref.at[me], turn_ref.at[me], local.at[1]),
    ]
    for copy in own:
        copy.start()
    fresh = []
    for d in range(1, TP):
        to = lax.rem(me + d, TP)
        copy = remote(f_ref.at[to], turn_ref.at[me], fsend.at[d], frecv.at[d], to)
        copy.start()
        fresh.append(copy)

    def push(src, origin, s, to, at):
        remote(src, out_ref.at[origin, s], send.at[at], recv.at[origin * 2 + s], to).start()

    def piece(origin, s):
        return out_ref.at[origin, s]

    def arrived(origin, s):
        remote(
            piece(origin, s), piece(origin, s), send.at[0], recv.at[origin * 2 + s], other_c
        ).wait_recv()

    def compute(origin, s):
        for part in range(2):
            scores = masked(out_ref, qa_ref, rows, ka_ref, origin, s, origin // 2, part)
            local_max[origin, pl.ds(s, 1), HALF * part : HALF * part + HALF] = jnp.max(
                scores, axis=0, keepdims=True
            )

    for s in range(2):
        for n, dz in enumerate((2, 1, 3)):
            push(q_ref.at[s], me, s, place(lax.rem(z + dz, ZS), y, c), s * 5 + n)
        push(q_ref.at[s], me, s, other_y, s * 5 + 3)
        push(q_ref.at[s], me, s, other_c, s * 5 + 4)
    for d in range(1, TP):
        fresh[d - 1].wait_recv()
    for copy in own:
        copy.wait()
    place_turns(turn_ref, rows, False)
    for s in range(2):
        each(KV_HEADS, lambda h: cache_copy(keys_ref, rows, loads, s, h).wait())
    each(2, lambda s: compute(me, s))

    def from_z(i):
        s = i // 3
        origin = place(lax.rem(z + 1 + lax.rem(i, 3), ZS), y, c)
        arrived(origin, s)
        push(piece(origin, s), origin, s, other_y, 10 + i)
        push(piece(origin, s), origin, s, other_c, 16 + i)
        compute(origin, s)

    each(6, from_z)

    def from_y(i):
        s = i // ZS
        origin = place(lax.rem(z + lax.rem(i, ZS), ZS), 1 - y, c)
        arrived(origin, s)
        push(piece(origin, s), origin, s, other_c, 22 + i)
        compute(origin, s)

    each(8, from_y)

    def from_c(i):
        s = lax.rem(i // ZS, 2)
        row = jnp.where(i < 8, y, 1 - y)
        origin = place(lax.rem(z + lax.rem(i, ZS), ZS), row, 1 - c)
        arrived(origin, s)
        compute(origin, s)

    each(16, from_c)
    firsts, seconds = [], []
    for d in range(1, TP):
        to = lax.rem(me + d, TP)
        copy = remote(local_max.at[to], slots.at[d - 1], msend.at[d], mrecv.at[d], to)
        copy.start()
        firsts.append(copy)
    best = local_max[me]
    for d in range(1, TP):
        firsts[d - 1].wait_recv()
        best = jnp.maximum(best, slots[d - 1])
    max_ref[me] = best
    for d in range(1, TP):
        to = lax.rem(me + d, TP)
        copy = remote(max_ref.at[me], max_ref.at[me], gsend.at[d], grecv.at[d], to)
        copy.start()
        seconds.append(copy)
    each(30, lambda i: remote(
        q_ref.at[0], out_ref.at[me, 0], send.at[i], recv.at[0], other_c
    ).wait_send())
    for copy in fresh + firsts:
        copy.wait_send()
    for copy in seconds:
        copy.wait()


def reduce_kernel(
    q_ref, turn_ref, max_ref, keys_ref, values_ref, ka_ref, qa_ref, out_ref,
    rows, vrows, num, sums, c_in, y_out, y_in, z_out, z_in, sums_in,
    loads, vloads, c_send, c_recv, y_send, y_recv, z_send, z_recv, l_send, l_recv,
):
    me = lax.axis_index("tp")
    c, y, z = lax.rem(me, 2), lax.rem(me // 2, 2), me // 4
    other_y, other_c = place(z, 1 - y, c), place(z, y, 1 - c)

    def ahead(i):
        return jnp.where(i == 0, 2, jnp.where(i == 1, 1, jnp.where(i == 2, 3, 0)))

    def chip(t):
        row = jnp.where(t < ZS, 1 - y, y)
        return lax.rem(z + ahead(lax.rem(t, ZS)), ZS) * 2 + row

    def load(t):
        h = chip(t)
        return [
            copy
            for s in range(2)
            for copy in (
                cache_copy(keys_ref, rows, loads, s, h),
                cache_copy(values_ref, vrows, vloads, s, h),
            )
        ]

    def start_load(t):
        for copy in load(t):
            copy.start()

    each(KV_HEADS, start_load)
    place_turns(turn_ref, rows, False)
    place_turns(turn_ref, vrows, True)
    greet(me)

    def c_copy(t, s):
        at = t * 2 + s
        return remote(
            num.at[chip(t) * 2 + 1 - c, s], c_in.at[at], c_send.at[at], c_recv.at[at], other_c
        )

    def y_copy(t, s):
        at = t * 2 + s
        return remote(y_out.at[at], y_in.at[at], y_send.at[at], y_recv.at[at], other_y)

    def z_copy(t, s):
        at = t * 2 + s
        to = place(lax.rem(z + ahead(t), ZS), y, c)
        return remote(z_out.at[at], z_in.at[at], z_send.at[at], z_recv.at[at], to)

    def compute(t):
        h = chip(t)
        for copy in load(t):
            copy.wait()

        def side(s):
            v = vrows[s, h].T
            for parity in range(2):
                dest = 2 * h + parity
                for part in range(2):
                    scores = masked(q_ref, qa_ref, rows, ka_ref, dest, s, h, part)
                    lanes = slice(HALF * part, HALF * part + HALF)
                    top = max_ref[dest, pl.ds(s, 1), lanes]
                    w = jnp.exp2((scores - top) * SCALE)
                    sums[dest, pl.ds(s, 1), lanes] = jnp.sum(w, axis=0, keepdims=True)
                    total = jnp.dot(
                        v, w.astype(jnp.bfloat16), preferred_element_type=jnp.float32
                    )
                    num[dest, s, lanes, :] = total.T

        each(2, side)
        for s in range(2):
            c_copy(t, s).start()

    def pass_y(t):
        for s in range(2):
            c_copy(t, s).wait_recv()
            at = t * 2 + s
            y_out[at] = (num[chip(t) * 2 + c, s] + c_in[at]).astype(jnp.bfloat16)
            y_copy(t, s).start()

    def summed(t, s):
        c_copy(t + ZS, s).wait_recv()
        y_copy(t, s).wait_recv()
        return (
            num[chip(t + ZS) * 2 + c, s]
            + c_in[(t + ZS) * 2 + s]
            + y_in[t * 2 + s].astype(jnp.float32)
        )

    def pass_z(t):
        for s in range(2):
            z_out[t * 2 + s] = summed(t, s).astype(jnp.bfloat16)
            z_copy(t, s).start()

    def step(t):
        compute(t)

        @pl.when((t >= 1) & (t <= ZS))
        def _():
            pass_y(t - 1)

        @pl.when(t > ZS)
        def _():
            pass_z(t - 1 - ZS)

    each(KV_HEADS, step)
    l_copies = []
    for d in range(1, TP):
        to = lax.rem(me + d, TP)
        copy = remote(sums.at[to], sums_in.at[d - 1], l_send.at[d], l_recv.at[d], to)
        copy.start()
        l_copies.append(copy)
    for s in range(2):
        c_in[6 + s] = summed(3, s)
    totals = sums[me]
    for d in range(1, TP):
        l_copies[d - 1].wait_recv()
        totals = totals + sums_in[d - 1]
    for s in range(2):
        for t in range(ZS - 1):
            z_copy(t, s).wait_recv()
        for j in range(WIDTH // 128):
            lanes = slice(128 * j, 128 * j + 128)
            column = jnp.broadcast_to(totals[s : s + 1, lanes], (128, 128)).T
            total = c_in[6 + s, lanes, :]
            for t in range(ZS - 1):
                total = total + z_in[t * 2 + s, lanes, :].astype(jnp.float32)
            out_ref[s, lanes, :] = (total / column).astype(jnp.bfloat16)
    for s in range(2):
        each(KV_HEADS, lambda t: c_copy(t, s).wait_send())
        each(ZS, lambda t: y_copy(t, s).wait_send())
        each(ZS - 1, lambda t: z_copy(t, s).wait_send())
    for copy in l_copies:
        copy.wait_send()


def visibility(prefill_prefixes, decode_prefixes, prefill_counts, me, query_rows, cache_rows):
    most = decode_prefixes.shape[0]
    turn_rows = query_rows // TP
    t = jnp.arange(most, dtype=jnp.int32)
    short = most - prefill_counts.shape[0]
    lengths = jnp.stack([jnp.pad(prefill_prefixes, (0, short)), decode_prefixes])
    counts = jnp.stack([jnp.pad(prefill_counts, (0, short)), jnp.full((most,), 2, jnp.int32)])
    both = jnp.stack([lengths, counts])
    ends = jnp.sum(jnp.where(t[None] <= t[:, None], both[:, :, None, :], 0), axis=-1)
    starts = ends - both
    at = me * cache_rows + jnp.arange(cache_rows, dtype=jnp.int32)
    cache = (at[None, :, None] >= starts[0][:, None]) & (at[None, :, None] < ends[0][:, None])
    cache = jnp.pad(cache, ((0, 0), (0, 0), (0, 128 - most)))
    line = jnp.arange(TURN_PAD, dtype=jnp.int32)
    side = jnp.arange(2, dtype=jnp.int32)[:, None]
    column = jnp.where(
        line[None] // turn_rows == side, most + me * turn_rows + line[None] % turn_rows, 127
    )
    lanes = jnp.arange(128, dtype=jnp.int32)
    turns = column[:, :, None] == lanes
    marks = jnp.concatenate([cache, turns], axis=1).astype(jnp.bfloat16)
    r = jnp.arange(query_rows, dtype=jnp.int32)
    mine = (r[None, :, None] >= starts[1][:, None]) & (r[None, :, None] < ends[1][:, None])
    first = jnp.sum(jnp.where(mine, starts[1][:, None], 0), axis=-1)
    j = lanes - most
    seen = (j >= first[:, :, None]) & (j <= r[None, :, None]) & (j >= 0)
    seen = seen | jnp.pad(mine, ((0, 0), (0, 0), (0, 128 - most)))
    hide = jnp.where(seen, 0.0, -1e30).astype(jnp.bfloat16)
    hide = jnp.broadcast_to(hide[:, :, None], (2, query_rows, 8, 128))
    return marks, hide.reshape(2, query_rows * 8, 128)


def fast_shards(
    queries,
    cache_keys,
    cache_values,
    fresh_keys,
    fresh_values,
    prefill_prefixes,
    decode_prefixes,
    prefill_counts,
):
    me = lax.axis_index("tp")
    query_rows = queries.shape[1]
    cache_rows = cache_keys.shape[1]
    turn_rows = query_rows // TP
    q = queries.reshape(2, query_rows * 8, HEAD_DIM)
    fresh = jnp.stack([fresh_keys, fresh_values]).reshape(2, 2, TP, turn_rows, -1)
    fresh = fresh.transpose(2, 0, 1, 3, 4).reshape(TP, 4 * turn_rows, -1)
    odd = lax.rem(me, 2) == 1
    zeros = jnp.zeros_like(fresh)
    fresh = jnp.concatenate(
        [jnp.where(odd, zeros, fresh), jnp.where(odd, fresh, zeros)], axis=2
    )
    marks, hide = visibility(
        prefill_prefixes, decode_prefixes, prefill_counts, me, query_rows, cache_rows
    )
    any_spec = pl.BlockSpec(memory_space=pl.ANY)
    vmem_spec = pl.BlockSpec(memory_space=pltpu.VMEM)
    dma = pltpu.SemaphoreType.DMA
    bf16, f32 = jnp.bfloat16, jnp.float32
    all_rows = pltpu.VMEM((2, KV_HEADS, cache_rows + TURN_PAD, HEAD_DIM), bf16)
    stats = (TP, 2, WIDTH)
    gathered, turns, row_max = pl.pallas_call(
        gather_kernel,
        out_shape=(
            jax.ShapeDtypeStruct((TP, *q.shape), bf16),
            jax.ShapeDtypeStruct(fresh.shape, bf16),
            jax.ShapeDtypeStruct(stats, f32),
        ),
        in_specs=[vmem_spec, vmem_spec, any_spec, vmem_spec, vmem_spec],
        out_specs=(vmem_spec,) * 3,
        scratch_shapes=[
            all_rows, pltpu.VMEM(stats, f32), pltpu.VMEM((TP - 1, 2, WIDTH), f32),
            dma((32,)), dma((32,)), dma((TP,)), dma((TP,)), dma((2,)), dma((16,)),
            dma((TP,)), dma((TP,)), dma((TP,)), dma((TP,)),
        ],
        compiler_params=pltpu.CompilerParams(
            collective_id=0, has_side_effects=True, vmem_limit_bytes=LIMIT
        ),
        name="gather_and_max",
    )(q, fresh, cache_keys, marks, hide)
    piece = (WIDTH, HEAD_DIM)
    attended = pl.pallas_call(
        reduce_kernel,
        out_shape=jax.ShapeDtypeStruct((2, *piece), bf16),
        in_specs=[vmem_spec] * 3 + [any_spec] * 2 + [vmem_spec] * 2,
        out_specs=vmem_spec,
        scratch_shapes=[
            all_rows, all_rows,
            pltpu.VMEM((TP, 2, *piece), f32),
            pltpu.VMEM(stats, f32),
            pltpu.VMEM((16, *piece), f32),
            pltpu.VMEM((8, *piece), bf16),
            pltpu.VMEM((8, *piece), bf16),
            pltpu.VMEM((6, *piece), bf16),
            pltpu.VMEM((6, *piece), bf16),
            pltpu.VMEM((TP - 1, 2, WIDTH), f32),
            dma((16,)), dma((16,)), dma((16,)), dma((16,)), dma((8,)), dma((8,)),
            dma((6,)), dma((6,)), dma((TP,)), dma((TP,)),
        ],
        compiler_params=pltpu.CompilerParams(
            collective_id=1, has_side_effects=True, vmem_limit_bytes=LIMIT
        ),
        name="weigh_and_reduce",
    )(gathered, turns, row_max, cache_keys, cache_values, marks, hide)
    shared = turns.reshape(KV_HEADS, 2, 2, 2, turn_rows, HEAD_DIM)
    shared = shared[:, 0] + shared[:, 1]
    handed = jnp.flip(shared.transpose(1, 2, 3, 0, 4), axis=1)
    handed = handed.reshape(2, 2, turn_rows, -1)
    return attended.reshape(queries.shape), handed[0], handed[1]


def solution(mesh):
    fast = mesh.shape["tp"] == TP and mesh.shape["role"] == 1
    return jax.shard_map(
        fast_shards if fast else shards,
        mesh=mesh,
        in_specs=(
            P(("groups", "role"), None, "tp"),
            P(("groups", "role"), "tp", None),
            P(("groups", "role"), "tp", None),
            P(("groups", "role"), None, "tp"),
            P(("groups", "role"), None, "tp"),
            P("groups"),
            P("groups"),
            P("groups"),
        ),
        out_specs=(
            P(("groups", "role"), None, "tp"),
            P(("groups", "role"), "tp", None),
            P(("groups", "role"), "tp", None),
        ),
        check_vma=False,
    )
```

```python
import math

import jax
import jax.numpy as jnp
from jax import lax
from jax.experimental import pallas as pl
from jax.experimental.pallas import tpu as pltpu
from jax.sharding import PartitionSpec as P

HEADS = 128
KV_HEADS = 8
HEAD_DIM = 128
GROUP_SIZE = 16


def passed_along(block, axis, distance):
    devices = range(lax.axis_size(axis))
    route = [((i - distance) % len(devices), i) for i in devices]
    return lax.ppermute(block, axis, route)


def owner_range(counts, start, length):
    ends = jnp.cumsum(counts)
    places = start + jnp.arange(length, dtype=jnp.int32)
    return jnp.sum((places[:, None] >= ends[None, :]).astype(jnp.int32), axis=1)


def masked_scores(grouped, key_block, visible):
    scores = jnp.einsum("qgad,kgd->gaqk", grouped, key_block, preferred_element_type=jnp.float32)
    scores = scores * HEAD_DIM ** (-0.5)
    return jnp.where(visible[None, None], scores, -1e30)


def shards(
    queries,
    cache_keys,
    cache_values,
    fresh_keys,
    fresh_values,
    prefill_prefixes,
    decode_prefixes,
    prefill_counts,
):
    device_place = lax.axis_index("tp")
    device_count = lax.axis_size("tp")
    side_place = lax.axis_index("role")
    local_sides = queries.shape[0]
    gathered = lax.all_gather(queries, "tp", axis=2, tiled=True)
    query_rows = gathered.shape[1]
    turn_keys, turn_values = (
        lax.all_to_all(fresh_keys, "tp", split_axis=1, concat_axis=2, tiled=True),
        lax.all_to_all(fresh_values, "tp", split_axis=1, concat_axis=2, tiled=True),
    )
    shifted_keys, shifted_values = passed_along((turn_keys, turn_values), "role", 1)
    handed_keys = jnp.flip(shifted_keys, axis=0)
    handed_values = jnp.flip(shifted_values, axis=0)
    query_places = jnp.arange(query_rows, dtype=jnp.int32)
    cache_rows = cache_keys.shape[1]
    cache_start = device_place * cache_rows
    turn_rows = turn_keys.shape[1]
    turn_places = device_place * turn_rows + jnp.arange(turn_rows, dtype=jnp.int32)
    block_rows = min(512, cache_rows)
    side_blocks = []
    side_grouped = []
    for local in range(local_sides):
        is_prefill = side_place * local_sides + local == 0
        query_owner = jnp.where(
            is_prefill, owner_range(prefill_counts, 0, query_rows), query_places // 2
        )
        cache_owner = jnp.where(
            is_prefill,
            owner_range(prefill_prefixes, cache_start, cache_rows),
            owner_range(decode_prefixes, cache_start, cache_rows),
        )
        turn_owner = jnp.where(
            is_prefill,
            owner_range(prefill_counts, device_place * turn_rows, turn_rows),
            turn_places // 2,
        )
        turn_visible = (query_owner[:, None] == turn_owner[None, :]) & (
            turn_places[None, :] <= query_places[:, None]
        )
        blocks = []
        for block_start in range(0, cache_rows, block_rows):
            key_block = cache_keys[local, block_start : block_start + block_rows].reshape(
                block_rows, KV_HEADS, HEAD_DIM
            )
            value_block = cache_values[local, block_start : block_start + block_rows].reshape(
                block_rows, KV_HEADS, HEAD_DIM
            )
            visible = (
                query_owner[:, None] == cache_owner[None, block_start : block_start + block_rows]
            )
            blocks.append((key_block, value_block, visible))
        blocks.append(
            (
                turn_keys[local].reshape(turn_rows, KV_HEADS, HEAD_DIM),
                turn_values[local].reshape(turn_rows, KV_HEADS, HEAD_DIM),
                turn_visible,
            )
        )
        side_blocks.append(blocks)
        side_grouped.append(gathered[local].reshape(query_rows, KV_HEADS, GROUP_SIZE, HEAD_DIM))
    maxima = []
    for local in range(local_sides):
        local_max = jnp.full((KV_HEADS, GROUP_SIZE, query_rows), -1e30, jnp.float32)
        for key_block, value_block, visible in side_blocks[local]:
            local_max = jnp.maximum(
                local_max, jnp.max(masked_scores(side_grouped[local], key_block, visible), axis=3)
            )
        maxima.append(local_max)
    row_max_all = lax.pmax(jnp.stack(maxima), "tp")
    numerators = []
    denominators = []
    for local in range(local_sides):
        row_max = row_max_all[local]
        numerator = jnp.zeros((query_rows, KV_HEADS, GROUP_SIZE, HEAD_DIM), jnp.float32)
        denominator = jnp.zeros((KV_HEADS, GROUP_SIZE, query_rows), jnp.float32)
        for key_block, value_block, visible in side_blocks[local]:
            weights = jnp.exp(
                masked_scores(side_grouped[local], key_block, visible) - row_max[..., None]
            )
            denominator = denominator + jnp.sum(weights, axis=3)
            numerator = numerator + jnp.einsum(
                "gaqk,kgd->qgad",
                weights.astype(jnp.bfloat16),
                value_block,
                preferred_element_type=jnp.float32,
            )
        numerators.append(numerator.reshape(query_rows, HEADS * HEAD_DIM))
        denominators.append(denominator.transpose(2, 0, 1).reshape(query_rows, HEADS))
    flat_numerator = jnp.stack(numerators)
    flat_denominator = jnp.stack(denominators)
    summed, totals = lax.psum((flat_numerator, flat_denominator), "tp")
    column_width = summed.shape[2] // device_count
    head_width = totals.shape[2] // device_count
    summed = lax.dynamic_slice_in_dim(summed, device_place * column_width, column_width, 2)
    totals = lax.dynamic_slice_in_dim(totals, device_place * head_width, head_width, 2)
    shares = summed.reshape(local_sides, query_rows, -1, HEAD_DIM) / totals[:, :, :, None]
    attended = shares.reshape(local_sides, query_rows, -1).astype(jnp.bfloat16)
    return (attended, handed_keys, handed_values)

TP = 16
ZS = 4
HALF = 256
WIDTH = 8 * 64
TURN_PAD = 16
SCALE = HEAD_DIM ** (-0.5) * math.log2(math.e)
MESH = pl.DeviceIdType.MESH
LIMIT = 56 * 1024 * 1024


def place(z, y, c):
    return (z * 2 + y) * 2 + c


def greet(me):
    barrier = pltpu.get_barrier_semaphore()
    for d in range(1, TP):
        pl.semaphore_signal(
            barrier, inc=1, device_id={"tp": lax.rem(me + d, TP)}, device_id_type=MESH
        )
    pl.semaphore_wait(barrier, TP - 1)


def remote(src, dst, send, recv, to):
    return pltpu.make_async_remote_copy(
        src_ref=src, dst_ref=dst, send_sem=send, recv_sem=recv,
        device_id={"tp": to}, device_id_type=MESH,
    )


def each(count, body):
    def step(i, carry):
        body(i)
        return carry

    lax.fori_loop(0, count, step, 0)


def cache_copy(cache_ref, rows_ref, sem, s, h):
    columns = pl.ds(pl.multiple_of(h * HEAD_DIM, HEAD_DIM), HEAD_DIM)
    count = cache_ref.shape[1]
    return pltpu.make_async_copy(
        cache_ref.at[s, :, columns], rows_ref.at[s, h, pl.ds(0, count), :], sem.at[s * KV_HEADS + h]
    )


def place_turns(turn_ref, rows_ref, values):
    count = rows_ref.shape[2] - TURN_PAD

    def body(h):
        rows = turn_ref[2 * h].astype(jnp.float32) + turn_ref[2 * h + 1].astype(jnp.float32)
        if values:
            rows = jnp.concatenate([rows[8:], rows[:8]], axis=0)
        for s in range(2):
            rows_ref[s, h, count:, :] = rows.astype(jnp.bfloat16)

    each(KV_HEADS, body)


def masked(q_ref, qa_ref, k_ref, ka_ref, origin, s, h, part):
    rows = slice(HALF * part, HALF * part + HALF)
    q = jnp.concatenate([q_ref[origin, s, rows, :], qa_ref[s, rows, :]], axis=1)
    k = jnp.concatenate([k_ref[s, h], ka_ref[s]], axis=1)
    return lax.dot_general(
        k, q, (((1,), (1,)), ((), ())), preferred_element_type=jnp.float32
    )


def attend_kernel(
    q_ref, f_ref, keys_ref, values_ref, ka_ref, qa_ref, attended_ref, turn_ref,
    out_ref, max_ref, rows, vrows, local_max, slots,
    num, sums, c_in, y_out, y_in, z_out, z_in, sums_in,
    send, recv, fsend, frecv, local, loads, vloads, msend, mrecv, gsend, grecv,
    c_send, c_recv, y_send, y_recv, z_send, z_recv, l_send, l_recv,
):
    me = lax.axis_index("tp")
    c, y, z = lax.rem(me, 2), lax.rem(me // 2, 2), me // 4
    other_y, other_c = place(z, 1 - y, c), place(z, y, 1 - c)
    for s in range(2):
        each(KV_HEADS, lambda h: cache_copy(keys_ref, rows, loads, s, h).start())
    for s in range(2):
        each(KV_HEADS, lambda h: cache_copy(values_ref, vrows, vloads, s, h).start())
    greet(me)
    own = [
        pltpu.make_async_copy(q_ref, out_ref.at[me], local.at[0]),
        pltpu.make_async_copy(f_ref.at[me], turn_ref.at[me], local.at[1]),
    ]
    for copy in own:
        copy.start()
    fresh = []
    for d in range(1, TP):
        to = lax.rem(me + d, TP)
        copy = remote(f_ref.at[to], turn_ref.at[me], fsend.at[d], frecv.at[d], to)
        copy.start()
        fresh.append(copy)

    def push(src, origin, s, to, at):
        remote(src, out_ref.at[origin, s], send.at[at], recv.at[origin * 2 + s], to).start()

    def piece(origin, s):
        return out_ref.at[origin, s]

    def arrived(origin, s):
        remote(
            piece(origin, s), piece(origin, s), send.at[0], recv.at[origin * 2 + s], other_c
        ).wait_recv()

    def compute(origin, s):
        for part in range(2):
            scores = masked(out_ref, qa_ref, rows, ka_ref, origin, s, origin // 2, part)
            local_max[origin, pl.ds(s, 1), HALF * part : HALF * part + HALF] = jnp.max(
                scores, axis=0, keepdims=True
            )

    def max_copy(d):
        to = lax.rem(me + d, TP)
        return remote(local_max.at[to], slots.at[d - 1], msend.at[d], mrecv.at[d], to)

    for s in range(2):
        for n, dz in enumerate((2, 1, 3)):
            push(q_ref.at[s], me, s, place(lax.rem(z + dz, ZS), y, c), s * 5 + n)
        push(q_ref.at[s], me, s, other_y, s * 5 + 3)
        push(q_ref.at[s], me, s, other_c, s * 5 + 4)
    for d in range(1, TP):
        fresh[d - 1].wait_recv()
    for copy in own:
        copy.wait()
    place_turns(turn_ref, rows, False)
    place_turns(turn_ref, vrows, True)
    for s in range(2):
        each(KV_HEADS, lambda h: cache_copy(keys_ref, rows, loads, s, h).wait())
    each(2, lambda s: compute(me, s))

    def nearest(i):
        return jnp.where(i == 2, 3, jnp.where(i == 3, 2, i))

    def from_z(i):
        s = i // 3
        origin = place(lax.rem(z + nearest(1 + lax.rem(i, 3)), ZS), y, c)
        arrived(origin, s)
        push(piece(origin, s), origin, s, other_y, 10 + i)
        push(piece(origin, s), origin, s, other_c, 16 + i)
        compute(origin, s)

        @pl.when(i >= 3)
        def _():
            max_copy(lax.rem(origin - me + TP, TP)).start()

    each(6, from_z)

    def from_y(i):
        s = i // ZS
        origin = place(lax.rem(z + nearest(lax.rem(i, ZS)), ZS), 1 - y, c)
        arrived(origin, s)
        push(piece(origin, s), origin, s, other_c, 22 + i)
        compute(origin, s)

        @pl.when(i >= ZS)
        def _():
            max_copy(lax.rem(origin - me + TP, TP)).start()

    each(8, from_y)

    def from_c(i):
        s = lax.rem(i // ZS, 2)
        row = jnp.where(i < 8, y, 1 - y)
        origin = place(lax.rem(z + nearest(lax.rem(i, ZS)), ZS), row, 1 - c)
        arrived(origin, s)
        compute(origin, s)

        @pl.when(lax.rem(i // ZS, 2) == 1)
        def _():
            max_copy(lax.rem(origin - me + TP, TP)).start()

    each(16, from_c)
    seconds = []
    best = local_max[me]
    for d in range(1, TP):
        max_copy(d).wait_recv()
        best = jnp.maximum(best, slots[d - 1])
    max_ref[me] = best
    for d in range(1, TP):
        to = lax.rem(me + d, TP)
        copy = remote(max_ref.at[me], max_ref.at[me], gsend.at[d], grecv.at[d], to)
        copy.start()
        seconds.append(copy)
    each(30, lambda i: remote(
        q_ref.at[0], out_ref.at[me, 0], send.at[i], recv.at[0], other_c
    ).wait_send())
    for copy in fresh:
        copy.wait_send()
    for d in range(1, TP):
        max_copy(d).wait_send()
    for copy in seconds:
        copy.wait()

    def ahead(i):
        return jnp.where(i == 0, 2, jnp.where(i == 1, 1, jnp.where(i == 2, 3, 0)))

    def chip(t):
        row = jnp.where(lax.rem(t, 2) == 0, 1 - y, y)
        return lax.rem(z + ahead(t // 2), ZS) * 2 + row

    def c_copy(t, s):
        at = t * 2 + s
        return remote(
            num.at[chip(t) * 2 + 1 - c, s], c_in.at[at], c_send.at[at], c_recv.at[at], other_c
        )

    def y_copy(t, s):
        at = t * 2 + s
        return remote(y_out.at[at], y_in.at[at], y_send.at[at], y_recv.at[at], other_y)

    def z_copy(t, s):
        at = t * 2 + s
        to = place(lax.rem(z + ahead(t), ZS), y, c)
        return remote(z_out.at[at], z_in.at[at], z_send.at[at], z_recv.at[at], to)

    def compute(t):
        h = chip(t)
        for s in range(2):
            cache_copy(values_ref, vrows, vloads, s, h).wait()

        def side(s):
            v = vrows[s, h].T
            for parity in range(2):
                dest = 2 * h + parity
                for part in range(2):
                    scores = masked(out_ref, qa_ref, rows, ka_ref, dest, s, h, part)
                    lanes = slice(HALF * part, HALF * part + HALF)
                    top = max_ref[dest, pl.ds(s, 1), lanes]
                    w = jnp.exp2((scores - top) * SCALE)
                    sums[dest, pl.ds(s, 1), lanes] = jnp.sum(w, axis=0, keepdims=True)
                    total = jnp.dot(
                        v, w.astype(jnp.bfloat16), preferred_element_type=jnp.float32
                    )
                    num[dest, s, lanes, :] = total.T

        each(2, side)
        for s in range(2):
            c_copy(t, s).start()

    def pass_y(t):
        for s in range(2):
            c_copy(2 * t, s).wait_recv()
            partial = num[chip(2 * t) * 2 + c, s] + c_in[4 * t + s]
            y_out[t * 2 + s] = partial.astype(jnp.bfloat16)
            y_copy(t, s).start()

    def summed(t, s):
        c_copy(2 * t + 1, s).wait_recv()
        y_copy(t, s).wait_recv()
        return (
            num[chip(2 * t + 1) * 2 + c, s]
            + c_in[4 * t + 2 + s]
            + y_in[t * 2 + s].astype(jnp.float32)
        )

    def pass_z(t):
        for s in range(2):
            z_out[t * 2 + s] = summed(t, s).astype(jnp.bfloat16)
            z_copy(t, s).start()

    def step(t):
        compute(2 * t)
        compute(2 * t + 1)
        pass_y(t)

        @pl.when(t >= 1)
        def _():
            pass_z(t - 1)

    each(ZS, step)
    l_copies = []
    for d in range(1, TP):
        to = lax.rem(me + d, TP)
        copy = remote(sums.at[to], sums_in.at[d - 1], l_send.at[d], l_recv.at[d], to)
        copy.start()
        l_copies.append(copy)
    for s in range(2):
        c_in[6 + s] = summed(3, s)
    totals = sums[me]
    for d in range(1, TP):
        l_copies[d - 1].wait_recv()
        totals = totals + sums_in[d - 1]
    for s in range(2):
        for t in range(ZS - 1):
            z_copy(t, s).wait_recv()
        for j in range(WIDTH // 128):
            lanes = slice(128 * j, 128 * j + 128)
            column = jnp.broadcast_to(totals[s : s + 1, lanes], (128, 128)).T
            total = c_in[6 + s, lanes, :]
            for t in range(ZS - 1):
                total = total + z_in[t * 2 + s, lanes, :].astype(jnp.float32)
            attended_ref[s, lanes, :] = (total / column).astype(jnp.bfloat16)
    for s in range(2):
        each(KV_HEADS, lambda t: c_copy(t, s).wait_send())
        each(ZS, lambda t: y_copy(t, s).wait_send())
        each(ZS - 1, lambda t: z_copy(t, s).wait_send())
    for copy in l_copies:
        copy.wait_send()


def visibility(prefill_prefixes, decode_prefixes, prefill_counts, me, query_rows, cache_rows):
    most = decode_prefixes.shape[0]
    turn_rows = query_rows // TP
    t = jnp.arange(most, dtype=jnp.int32)
    short = most - prefill_counts.shape[0]
    lengths = jnp.stack([jnp.pad(prefill_prefixes, (0, short)), decode_prefixes])
    counts = jnp.stack([jnp.pad(prefill_counts, (0, short)), jnp.full((most,), 2, jnp.int32)])
    both = jnp.stack([lengths, counts])
    ends = jnp.sum(jnp.where(t[None] <= t[:, None], both[:, :, None, :], 0), axis=-1)
    starts = ends - both
    at = me * cache_rows + jnp.arange(cache_rows, dtype=jnp.int32)
    cache = (at[None, :, None] >= starts[0][:, None]) & (at[None, :, None] < ends[0][:, None])
    cache = jnp.pad(cache, ((0, 0), (0, 0), (0, 128 - most)))
    line = jnp.arange(TURN_PAD, dtype=jnp.int32)
    side = jnp.arange(2, dtype=jnp.int32)[:, None]
    column = jnp.where(
        line[None] // turn_rows == side, most + me * turn_rows + line[None] % turn_rows, 127
    )
    lanes = jnp.arange(128, dtype=jnp.int32)
    turns = column[:, :, None] == lanes
    marks = jnp.concatenate([cache, turns], axis=1).astype(jnp.bfloat16)
    r = jnp.arange(query_rows, dtype=jnp.int32)
    mine = (r[None, :, None] >= starts[1][:, None]) & (r[None, :, None] < ends[1][:, None])
    first = jnp.sum(jnp.where(mine, starts[1][:, None], 0), axis=-1)
    j = lanes - most
    seen = (j >= first[:, :, None]) & (j <= r[None, :, None]) & (j >= 0)
    seen = seen | jnp.pad(mine, ((0, 0), (0, 0), (0, 128 - most)))
    hide = jnp.where(seen, 0.0, -1e30).astype(jnp.bfloat16)
    hide = jnp.broadcast_to(hide[:, :, None], (2, query_rows, 8, 128))
    return marks, hide.reshape(2, query_rows * 8, 128)


def fast_shards(
    queries,
    cache_keys,
    cache_values,
    fresh_keys,
    fresh_values,
    prefill_prefixes,
    decode_prefixes,
    prefill_counts,
):
    me = lax.axis_index("tp")
    query_rows = queries.shape[1]
    cache_rows = cache_keys.shape[1]
    turn_rows = query_rows // TP
    q = queries.reshape(2, query_rows * 8, HEAD_DIM)
    fresh = jnp.stack([fresh_keys, fresh_values]).reshape(2, 2, TP, turn_rows, -1)
    fresh = fresh.transpose(2, 0, 1, 3, 4).reshape(TP, 4 * turn_rows, -1)
    odd = lax.rem(me, 2) == 1
    zeros = jnp.zeros_like(fresh)
    fresh = jnp.concatenate(
        [jnp.where(odd, zeros, fresh), jnp.where(odd, fresh, zeros)], axis=2
    )
    marks, hide = visibility(
        prefill_prefixes, decode_prefixes, prefill_counts, me, query_rows, cache_rows
    )
    any_spec = pl.BlockSpec(memory_space=pl.ANY)
    vmem_spec = pl.BlockSpec(memory_space=pltpu.VMEM)
    dma = pltpu.SemaphoreType.DMA
    bf16, f32 = jnp.bfloat16, jnp.float32
    all_rows = pltpu.VMEM((2, KV_HEADS, cache_rows + TURN_PAD, HEAD_DIM), bf16)
    stats = (TP, 2, WIDTH)
    piece = (WIDTH, HEAD_DIM)
    attended, turns = pl.pallas_call(
        attend_kernel,
        out_shape=(
            jax.ShapeDtypeStruct((2, *piece), bf16),
            jax.ShapeDtypeStruct(fresh.shape, bf16),
        ),
        in_specs=[vmem_spec, vmem_spec, any_spec, any_spec, vmem_spec, vmem_spec],
        out_specs=(vmem_spec,) * 2,
        scratch_shapes=[
            pltpu.VMEM((TP, *q.shape), bf16), pltpu.VMEM(stats, f32),
            all_rows, all_rows,
            pltpu.VMEM(stats, f32), pltpu.VMEM((TP - 1, 2, WIDTH), f32),
            pltpu.VMEM((TP, 2, *piece), f32),
            pltpu.VMEM(stats, f32),
            pltpu.VMEM((16, *piece), f32),
            pltpu.VMEM((8, *piece), bf16),
            pltpu.VMEM((8, *piece), bf16),
            pltpu.VMEM((6, *piece), bf16),
            pltpu.VMEM((6, *piece), bf16),
            pltpu.VMEM((TP - 1, 2, WIDTH), f32),
            dma((32,)), dma((32,)), dma((TP,)), dma((TP,)), dma((2,)), dma((16,)),
            dma((16,)), dma((TP,)), dma((TP,)), dma((TP,)), dma((TP,)),
            dma((16,)), dma((16,)), dma((8,)), dma((8,)),
            dma((6,)), dma((6,)), dma((TP,)), dma((TP,)),
        ],
        compiler_params=pltpu.CompilerParams(
            collective_id=0, has_side_effects=True, vmem_limit_bytes=LIMIT
        ),
        name="attend",
    )(q, fresh, cache_keys, cache_values, marks, hide)
    shared = turns.reshape(KV_HEADS, 2, 2, 2, turn_rows, HEAD_DIM)
    shared = shared[:, 0] + shared[:, 1]
    handed = jnp.flip(shared.transpose(1, 2, 3, 0, 4), axis=1)
    handed = handed.reshape(2, 2, turn_rows, -1)
    return attended.reshape(queries.shape), handed[0], handed[1]


def solution(mesh):
    fast = mesh.shape["tp"] == TP and mesh.shape["role"] == 1
    return jax.shard_map(
        fast_shards if fast else shards,
        mesh=mesh,
        in_specs=(
            P(("groups", "role"), None, "tp"),
            P(("groups", "role"), "tp", None),
            P(("groups", "role"), "tp", None),
            P(("groups", "role"), None, "tp"),
            P(("groups", "role"), None, "tp"),
            P("groups"),
            P("groups"),
            P("groups"),
        ),
        out_specs=(
            P(("groups", "role"), None, "tp"),
            P(("groups", "role"), "tp", None),
            P(("groups", "role"), "tp", None),
        ),
        check_vma=False,
    )
```

```python
import math

import jax
import jax.numpy as jnp
from jax import lax
from jax.experimental import pallas as pl
from jax.experimental.pallas import tpu as pltpu
from jax.sharding import PartitionSpec as P

HEADS = 128
KV_HEADS = 8
HEAD_DIM = 128
GROUP_SIZE = 16


def passed_along(block, axis, distance):
    devices = range(lax.axis_size(axis))
    route = [((i - distance) % len(devices), i) for i in devices]
    return lax.ppermute(block, axis, route)


def owner_range(counts, start, length):
    ends = jnp.cumsum(counts)
    places = start + jnp.arange(length, dtype=jnp.int32)
    return jnp.sum((places[:, None] >= ends[None, :]).astype(jnp.int32), axis=1)


def masked_scores(grouped, key_block, visible):
    scores = jnp.einsum("qgad,kgd->gaqk", grouped, key_block, preferred_element_type=jnp.float32)
    scores = scores * HEAD_DIM ** (-0.5)
    return jnp.where(visible[None, None], scores, -1e30)


def shards(
    queries,
    cache_keys,
    cache_values,
    fresh_keys,
    fresh_values,
    prefill_prefixes,
    decode_prefixes,
    prefill_counts,
):
    device_place = lax.axis_index("tp")
    device_count = lax.axis_size("tp")
    side_place = lax.axis_index("role")
    local_sides = queries.shape[0]
    gathered = lax.all_gather(queries, "tp", axis=2, tiled=True)
    query_rows = gathered.shape[1]
    turn_keys, turn_values = (
        lax.all_to_all(fresh_keys, "tp", split_axis=1, concat_axis=2, tiled=True),
        lax.all_to_all(fresh_values, "tp", split_axis=1, concat_axis=2, tiled=True),
    )
    shifted_keys, shifted_values = passed_along((turn_keys, turn_values), "role", 1)
    handed_keys = jnp.flip(shifted_keys, axis=0)
    handed_values = jnp.flip(shifted_values, axis=0)
    query_places = jnp.arange(query_rows, dtype=jnp.int32)
    cache_rows = cache_keys.shape[1]
    cache_start = device_place * cache_rows
    turn_rows = turn_keys.shape[1]
    turn_places = device_place * turn_rows + jnp.arange(turn_rows, dtype=jnp.int32)
    block_rows = min(512, cache_rows)
    side_blocks = []
    side_grouped = []
    for local in range(local_sides):
        is_prefill = side_place * local_sides + local == 0
        query_owner = jnp.where(
            is_prefill, owner_range(prefill_counts, 0, query_rows), query_places // 2
        )
        cache_owner = jnp.where(
            is_prefill,
            owner_range(prefill_prefixes, cache_start, cache_rows),
            owner_range(decode_prefixes, cache_start, cache_rows),
        )
        turn_owner = jnp.where(
            is_prefill,
            owner_range(prefill_counts, device_place * turn_rows, turn_rows),
            turn_places // 2,
        )
        turn_visible = (query_owner[:, None] == turn_owner[None, :]) & (
            turn_places[None, :] <= query_places[:, None]
        )
        blocks = []
        for block_start in range(0, cache_rows, block_rows):
            key_block = cache_keys[local, block_start : block_start + block_rows].reshape(
                block_rows, KV_HEADS, HEAD_DIM
            )
            value_block = cache_values[local, block_start : block_start + block_rows].reshape(
                block_rows, KV_HEADS, HEAD_DIM
            )
            visible = (
                query_owner[:, None] == cache_owner[None, block_start : block_start + block_rows]
            )
            blocks.append((key_block, value_block, visible))
        blocks.append(
            (
                turn_keys[local].reshape(turn_rows, KV_HEADS, HEAD_DIM),
                turn_values[local].reshape(turn_rows, KV_HEADS, HEAD_DIM),
                turn_visible,
            )
        )
        side_blocks.append(blocks)
        side_grouped.append(gathered[local].reshape(query_rows, KV_HEADS, GROUP_SIZE, HEAD_DIM))
    maxima = []
    for local in range(local_sides):
        local_max = jnp.full((KV_HEADS, GROUP_SIZE, query_rows), -1e30, jnp.float32)
        for key_block, value_block, visible in side_blocks[local]:
            local_max = jnp.maximum(
                local_max, jnp.max(masked_scores(side_grouped[local], key_block, visible), axis=3)
            )
        maxima.append(local_max)
    row_max_all = lax.pmax(jnp.stack(maxima), "tp")
    numerators = []
    denominators = []
    for local in range(local_sides):
        row_max = row_max_all[local]
        numerator = jnp.zeros((query_rows, KV_HEADS, GROUP_SIZE, HEAD_DIM), jnp.float32)
        denominator = jnp.zeros((KV_HEADS, GROUP_SIZE, query_rows), jnp.float32)
        for key_block, value_block, visible in side_blocks[local]:
            weights = jnp.exp(
                masked_scores(side_grouped[local], key_block, visible) - row_max[..., None]
            )
            denominator = denominator + jnp.sum(weights, axis=3)
            numerator = numerator + jnp.einsum(
                "gaqk,kgd->qgad",
                weights.astype(jnp.bfloat16),
                value_block,
                preferred_element_type=jnp.float32,
            )
        numerators.append(numerator.reshape(query_rows, HEADS * HEAD_DIM))
        denominators.append(denominator.transpose(2, 0, 1).reshape(query_rows, HEADS))
    flat_numerator = jnp.stack(numerators)
    flat_denominator = jnp.stack(denominators)
    summed, totals = lax.psum((flat_numerator, flat_denominator), "tp")
    column_width = summed.shape[2] // device_count
    head_width = totals.shape[2] // device_count
    summed = lax.dynamic_slice_in_dim(summed, device_place * column_width, column_width, 2)
    totals = lax.dynamic_slice_in_dim(totals, device_place * head_width, head_width, 2)
    shares = summed.reshape(local_sides, query_rows, -1, HEAD_DIM) / totals[:, :, :, None]
    attended = shares.reshape(local_sides, query_rows, -1).astype(jnp.bfloat16)
    return (attended, handed_keys, handed_values)

TP = 16
ZS = 4
HALF = 256
WIDTH = 8 * 64
TURN_PAD = 16
SCALE = HEAD_DIM ** (-0.5) * math.log2(math.e)
MESH = pl.DeviceIdType.MESH
LIMIT = 56 * 1024 * 1024


def place(z, y, c):
    return (z * 2 + y) * 2 + c


def greet(me):
    barrier = pltpu.get_barrier_semaphore()
    for d in range(1, TP):
        pl.semaphore_signal(
            barrier, inc=1, device_id={"tp": lax.rem(me + d, TP)}, device_id_type=MESH
        )
    pl.semaphore_wait(barrier, TP - 1)


def remote(src, dst, send, recv, to):
    return pltpu.make_async_remote_copy(
        src_ref=src, dst_ref=dst, send_sem=send, recv_sem=recv,
        device_id={"tp": to}, device_id_type=MESH,
    )


def each(count, body):
    def step(i, carry):
        body(i)
        return carry

    lax.fori_loop(0, count, step, 0)


def cache_copy(cache_ref, rows_ref, sem, s, h):
    columns = pl.ds(pl.multiple_of(h * HEAD_DIM, HEAD_DIM), HEAD_DIM)
    count = cache_ref.shape[1]
    return pltpu.make_async_copy(
        cache_ref.at[s, :, columns], rows_ref.at[s, h, pl.ds(0, count), :], sem.at[s * KV_HEADS + h]
    )


def place_turns(turn_ref, rows_ref, values):
    count = rows_ref.shape[2] - TURN_PAD

    def body(h):
        rows = turn_ref[2 * h].astype(jnp.float32) + turn_ref[2 * h + 1].astype(jnp.float32)
        if values:
            rows = jnp.concatenate([rows[8:], rows[:8]], axis=0)
        for s in range(2):
            rows_ref[s, h, count:, :] = rows.astype(jnp.bfloat16)

    each(KV_HEADS, body)


def masked(q_ref, qa_ref, k_ref, ka_ref, origin, s, h, part):
    rows = slice(HALF * part, HALF * part + HALF)
    q = jnp.concatenate([q_ref[origin, s, rows, :], qa_ref[s, rows, :]], axis=1)
    k = jnp.concatenate([k_ref[s, h], ka_ref[s]], axis=1)
    return lax.dot_general(
        k, q, (((1,), (1,)), ((), ())), preferred_element_type=jnp.float32
    )


def attend_kernel(
    q_ref, f_ref, keys_ref, values_ref, ka_ref, qa_ref, attended_ref, turn_ref,
    out_ref, max_ref, rows, vrows, local_max, slots,
    num, sums, c_in, y_out, y_in, z_out, z_in, sums_in,
    send, recv, fsend, frecv, local, loads, vloads, msend, mrecv, gsend, grecv,
    c_send, c_recv, y_send, y_recv, z_send, z_recv, l_send, l_recv,
):
    me = lax.axis_index("tp")
    c, y, z = lax.rem(me, 2), lax.rem(me // 2, 2), me // 4
    other_y, other_c = place(z, 1 - y, c), place(z, y, 1 - c)
    for s in range(2):
        each(KV_HEADS, lambda h: cache_copy(keys_ref, rows, loads, s, h).start())
    for s in range(2):
        each(KV_HEADS, lambda h: cache_copy(values_ref, vrows, vloads, s, h).start())
    greet(me)
    own = [
        pltpu.make_async_copy(q_ref, out_ref.at[me], local.at[0]),
        pltpu.make_async_copy(f_ref.at[me], turn_ref.at[me], local.at[1]),
    ]
    for copy in own:
        copy.start()
    fresh = []
    for d in range(1, TP):
        to = lax.rem(me + d, TP)
        copy = remote(f_ref.at[to], turn_ref.at[me], fsend.at[d], frecv.at[d], to)
        copy.start()
        fresh.append(copy)

    def push(src, origin, s, to, at):
        remote(src, out_ref.at[origin, s], send.at[at], recv.at[origin * 2 + s], to).start()

    def piece(origin, s):
        return out_ref.at[origin, s]

    def arrived(origin, s):
        remote(
            piece(origin, s), piece(origin, s), send.at[0], recv.at[origin * 2 + s], other_c
        ).wait_recv()

    def compute(origin, s):
        for part in range(2):
            scores = masked(out_ref, qa_ref, rows, ka_ref, origin, s, origin // 2, part)
            local_max[origin, pl.ds(s, 1), HALF * part : HALF * part + HALF] = jnp.max(
                scores, axis=0, keepdims=True
            )

    def max_copy(d):
        to = lax.rem(me + d, TP)
        return remote(local_max.at[to], slots.at[d - 1], msend.at[d], mrecv.at[d], to)

    for s in range(2):
        for n, dz in enumerate((2, 1, 3)):
            push(q_ref.at[s], me, s, place(lax.rem(z + dz, ZS), y, c), s * 5 + n)
        push(q_ref.at[s], me, s, other_y, s * 5 + 3)
        push(q_ref.at[s], me, s, other_c, s * 5 + 4)
    for d in range(1, TP):
        fresh[d - 1].wait_recv()
    for copy in own:
        copy.wait()
    place_turns(turn_ref, rows, False)
    place_turns(turn_ref, vrows, True)
    for s in range(2):
        each(KV_HEADS, lambda h: cache_copy(keys_ref, rows, loads, s, h).wait())
    each(2, lambda s: compute(me, s))

    def nearest(i):
        return jnp.where(i == 2, 3, jnp.where(i == 3, 2, i))

    def from_z(i):
        s = i // 3
        origin = place(lax.rem(z + nearest(1 + lax.rem(i, 3)), ZS), y, c)
        arrived(origin, s)
        push(piece(origin, s), origin, s, other_y, 10 + i)
        push(piece(origin, s), origin, s, other_c, 16 + i)
        compute(origin, s)

        @pl.when(i >= 3)
        def _():
            max_copy(lax.rem(origin - me + TP, TP)).start()

    def along(i):
        return lax.rem(z + nearest(i), ZS)

    def finish(origin, s):
        compute(origin, s)

        @pl.when(s == 1)
        def _():
            max_copy(lax.rem(origin - me + TP, TP)).start()

    def take_y(origin, s, at):
        arrived(origin, s)
        push(piece(origin, s), origin, s, other_c, at)
        finish(origin, s)

    def take_c(origin, s):
        arrived(origin, s)
        finish(origin, s)

    each(2, lambda s: take_y(other_y, s, 22 + s))
    each(2, lambda s: take_c(other_c, s))
    each(6, from_z)
    each(6, lambda i: take_y(place(along(1 + lax.rem(i, 3)), 1 - y, c), i // 3, 24 + i))
    each(6, lambda i: take_c(place(along(1 + lax.rem(i, 3)), y, 1 - c), i // 3))
    each(8, lambda i: take_c(place(along(lax.rem(i, ZS)), 1 - y, 1 - c), i // ZS))
    seconds = []
    best = local_max[me]
    for d in range(1, TP):
        max_copy(d).wait_recv()
        best = jnp.maximum(best, slots[d - 1])
    max_ref[me] = best
    for d in range(1, TP):
        to = lax.rem(me + d, TP)
        copy = remote(max_ref.at[me], max_ref.at[me], gsend.at[d], grecv.at[d], to)
        copy.start()
        seconds.append(copy)
    each(30, lambda i: remote(
        q_ref.at[0], out_ref.at[me, 0], send.at[i], recv.at[0], other_c
    ).wait_send())
    for copy in fresh:
        copy.wait_send()
    for d in range(1, TP):
        max_copy(d).wait_send()

    def ahead(i):
        return jnp.where(i == 0, 2, jnp.where(i == 1, 1, jnp.where(i == 2, 3, 0)))

    def chip(t):
        row = jnp.where(lax.rem(t, 2) == 0, 1 - y, y)
        return lax.rem(z + ahead(t // 2), ZS) * 2 + row

    def c_copy(t, s):
        at = t * 2 + s
        return remote(
            num.at[chip(t) * 2 + 1 - c, s], c_in.at[at], c_send.at[at], c_recv.at[at], other_c
        )

    def y_copy(t, s):
        at = t * 2 + s
        return remote(y_out.at[at], y_in.at[at], y_send.at[at], y_recv.at[at], other_y)

    def z_copy(t, s):
        at = t * 2 + s
        to = place(lax.rem(z + ahead(t), ZS), y, c)
        return remote(z_out.at[at], z_in.at[at], z_send.at[at], z_recv.at[at], to)

    def compute(t):
        h = chip(t)
        for s in range(2):
            cache_copy(values_ref, vrows, vloads, s, h).wait()
        for core in range(2):
            src = 2 * h + core
            d = lax.rem(me - src + TP, TP)

            @pl.when(d != 0)
            def _():
                remote(
                    max_ref.at[src], max_ref.at[src], gsend.at[d], grecv.at[d], other_c
                ).wait_recv()

        def side(s):
            v = vrows[s, h].T
            for parity in range(2):
                dest = 2 * h + parity
                for part in range(2):
                    scores = masked(out_ref, qa_ref, rows, ka_ref, dest, s, h, part)
                    lanes = slice(HALF * part, HALF * part + HALF)
                    top = max_ref[dest, pl.ds(s, 1), lanes]
                    w = jnp.exp2((scores - top) * SCALE)
                    sums[dest, pl.ds(s, 1), lanes] = jnp.sum(w, axis=0, keepdims=True)
                    total = jnp.dot(
                        v, w.astype(jnp.bfloat16), preferred_element_type=jnp.float32
                    )
                    num[dest, s, lanes, :] = total.T

        each(2, side)
        for s in range(2):
            c_copy(t, s).start()

    def pass_y(t):
        for s in range(2):
            c_copy(2 * t, s).wait_recv()
            partial = num[chip(2 * t) * 2 + c, s] + c_in[4 * t + s]
            y_out[t * 2 + s] = partial.astype(jnp.bfloat16)
            y_copy(t, s).start()

    def summed(t, s):
        c_copy(2 * t + 1, s).wait_recv()
        y_copy(t, s).wait_recv()
        return (
            num[chip(2 * t + 1) * 2 + c, s]
            + c_in[4 * t + 2 + s]
            + y_in[t * 2 + s].astype(jnp.float32)
        )

    def pass_z(t):
        for s in range(2):
            z_out[t * 2 + s] = summed(t, s).astype(jnp.bfloat16)
            z_copy(t, s).start()

    def step(t):
        compute(2 * t)
        compute(2 * t + 1)
        pass_y(t)

        @pl.when(t >= 1)
        def _():
            pass_z(t - 1)

    each(ZS, step)
    l_copies = []
    for d in range(1, TP):
        to = lax.rem(me + d, TP)
        copy = remote(sums.at[to], sums_in.at[d - 1], l_send.at[d], l_recv.at[d], to)
        copy.start()
        l_copies.append(copy)
    for s in range(2):
        c_in[6 + s] = summed(3, s)
    totals = sums[me]
    for d in range(1, TP):
        l_copies[d - 1].wait_recv()
        totals = totals + sums_in[d - 1]
    for s in range(2):
        for t in range(ZS - 1):
            z_copy(t, s).wait_recv()
        for j in range(WIDTH // 128):
            lanes = slice(128 * j, 128 * j + 128)
            column = jnp.broadcast_to(totals[s : s + 1, lanes], (128, 128)).T
            total = c_in[6 + s, lanes, :]
            for t in range(ZS - 1):
                total = total + z_in[t * 2 + s, lanes, :].astype(jnp.float32)
            attended_ref[s, lanes, :] = (total / column).astype(jnp.bfloat16)
    for s in range(2):
        each(KV_HEADS, lambda t: c_copy(t, s).wait_send())
        each(ZS, lambda t: y_copy(t, s).wait_send())
        each(ZS - 1, lambda t: z_copy(t, s).wait_send())
    for copy in l_copies + seconds:
        copy.wait_send()


def visibility(prefill_prefixes, decode_prefixes, prefill_counts, me, query_rows, cache_rows):
    most = decode_prefixes.shape[0]
    turn_rows = query_rows // TP
    t = jnp.arange(most, dtype=jnp.int32)
    short = most - prefill_counts.shape[0]
    lengths = jnp.stack([jnp.pad(prefill_prefixes, (0, short)), decode_prefixes])
    counts = jnp.stack([jnp.pad(prefill_counts, (0, short)), jnp.full((most,), 2, jnp.int32)])
    both = jnp.stack([lengths, counts])
    ends = jnp.sum(jnp.where(t[None] <= t[:, None], both[:, :, None, :], 0), axis=-1)
    starts = ends - both
    at = me * cache_rows + jnp.arange(cache_rows, dtype=jnp.int32)
    cache = (at[None, :, None] >= starts[0][:, None]) & (at[None, :, None] < ends[0][:, None])
    cache = jnp.pad(cache, ((0, 0), (0, 0), (0, 128 - most)))
    line = jnp.arange(TURN_PAD, dtype=jnp.int32)
    side = jnp.arange(2, dtype=jnp.int32)[:, None]
    column = jnp.where(
        line[None] // turn_rows == side, most + me * turn_rows + line[None] % turn_rows, 127
    )
    lanes = jnp.arange(128, dtype=jnp.int32)
    turns = column[:, :, None] == lanes
    marks = jnp.concatenate([cache, turns], axis=1).astype(jnp.bfloat16)
    r = jnp.arange(query_rows, dtype=jnp.int32)
    mine = (r[None, :, None] >= starts[1][:, None]) & (r[None, :, None] < ends[1][:, None])
    first = jnp.sum(jnp.where(mine, starts[1][:, None], 0), axis=-1)
    j = lanes - most
    seen = (j >= first[:, :, None]) & (j <= r[None, :, None]) & (j >= 0)
    seen = seen | jnp.pad(mine, ((0, 0), (0, 0), (0, 128 - most)))
    hide = jnp.where(seen, 0.0, -1e30).astype(jnp.bfloat16)
    hide = jnp.broadcast_to(hide[:, :, None], (2, query_rows, 8, 128))
    return marks, hide.reshape(2, query_rows * 8, 128)


def fast_shards(
    queries,
    cache_keys,
    cache_values,
    fresh_keys,
    fresh_values,
    prefill_prefixes,
    decode_prefixes,
    prefill_counts,
):
    me = lax.axis_index("tp")
    query_rows = queries.shape[1]
    cache_rows = cache_keys.shape[1]
    turn_rows = query_rows // TP
    q = queries.reshape(2, query_rows * 8, HEAD_DIM)
    fresh = jnp.stack([fresh_keys, fresh_values]).reshape(2, 2, TP, turn_rows, -1)
    fresh = fresh.transpose(2, 0, 1, 3, 4).reshape(TP, 4 * turn_rows, -1)
    odd = lax.rem(me, 2) == 1
    zeros = jnp.zeros_like(fresh)
    fresh = jnp.concatenate(
        [jnp.where(odd, zeros, fresh), jnp.where(odd, fresh, zeros)], axis=2
    )
    marks, hide = visibility(
        prefill_prefixes, decode_prefixes, prefill_counts, me, query_rows, cache_rows
    )
    any_spec = pl.BlockSpec(memory_space=pl.ANY)
    vmem_spec = pl.BlockSpec(memory_space=pltpu.VMEM)
    dma = pltpu.SemaphoreType.DMA
    bf16, f32 = jnp.bfloat16, jnp.float32
    all_rows = pltpu.VMEM((2, KV_HEADS, cache_rows + TURN_PAD, HEAD_DIM), bf16)
    stats = (TP, 2, WIDTH)
    piece = (WIDTH, HEAD_DIM)
    attended, turns = pl.pallas_call(
        attend_kernel,
        out_shape=(
            jax.ShapeDtypeStruct((2, *piece), bf16),
            jax.ShapeDtypeStruct(fresh.shape, bf16),
        ),
        in_specs=[vmem_spec, vmem_spec, any_spec, any_spec, vmem_spec, vmem_spec],
        out_specs=(vmem_spec,) * 2,
        scratch_shapes=[
            pltpu.VMEM((TP, *q.shape), bf16), pltpu.VMEM(stats, f32),
            all_rows, all_rows,
            pltpu.VMEM(stats, f32), pltpu.VMEM((TP - 1, 2, WIDTH), f32),
            pltpu.VMEM((TP, 2, *piece), f32),
            pltpu.VMEM(stats, f32),
            pltpu.VMEM((16, *piece), f32),
            pltpu.VMEM((8, *piece), bf16),
            pltpu.VMEM((8, *piece), bf16),
            pltpu.VMEM((6, *piece), bf16),
            pltpu.VMEM((6, *piece), bf16),
            pltpu.VMEM((TP - 1, 2, WIDTH), f32),
            dma((32,)), dma((32,)), dma((TP,)), dma((TP,)), dma((2,)), dma((16,)),
            dma((16,)), dma((TP,)), dma((TP,)), dma((TP,)), dma((TP,)),
            dma((16,)), dma((16,)), dma((8,)), dma((8,)),
            dma((6,)), dma((6,)), dma((TP,)), dma((TP,)),
        ],
        compiler_params=pltpu.CompilerParams(
            collective_id=0, has_side_effects=True, vmem_limit_bytes=LIMIT
        ),
        name="attend",
    )(q, fresh, cache_keys, cache_values, marks, hide)
    shared = turns.reshape(KV_HEADS, 2, 2, 2, turn_rows, HEAD_DIM)
    shared = shared[:, 0] + shared[:, 1]
    handed = jnp.flip(shared.transpose(1, 2, 3, 0, 4), axis=1)
    handed = handed.reshape(2, 2, turn_rows, -1)
    return attended.reshape(queries.shape), handed[0], handed[1]


def solution(mesh):
    fast = mesh.shape["tp"] == TP and mesh.shape["role"] == 1
    return jax.shard_map(
        fast_shards if fast else shards,
        mesh=mesh,
        in_specs=(
            P(("groups", "role"), None, "tp"),
            P(("groups", "role"), "tp", None),
            P(("groups", "role"), "tp", None),
            P(("groups", "role"), None, "tp"),
            P(("groups", "role"), None, "tp"),
            P("groups"),
            P("groups"),
            P("groups"),
        ),
        out_specs=(
            P(("groups", "role"), None, "tp"),
            P(("groups", "role"), "tp", None),
            P(("groups", "role"), "tp", None),
        ),
        check_vma=False,
    )
```
